512 devices in a mesh: gx: 8 (over x, core), gy: 16 (over z), gz: 4 (over y).
Axes of the slice: x: 4, y: 4, z: 16, core: 2. Of those that a mesh axis runs over, the one named last changes fastest.
Arguments:
- gradient: bfloat16 [8, 2048, 8192], P('gx', ('gy', 'gz')), may hold values from -1000 to 1000, as said below
- error_buffer: bfloat16 [8, 2048, 8192], P('gx', ('gy', 'gz')), may hold values from -6 to 6
- warm_factor: float32 [32, 2048], P(None, ('gy', 'gz')), may hold values from -6 to 6
Outputs:
- applied_update: bfloat16 [2048, 8192], P(('gy', 'gz'))
- next_error: bfloat16 [8, 2048, 8192], P('gx', ('gy', 'gz'))
- next_factor: float32 [32, 2048], P(None, ('gy', 'gz'))
The draws below stay inside these ranges and needn't reach their ends.
Inputs may be any that keep to these rules, and one draw needn't show every extreme that they name: Real-valued gradient entries.
All inputs are finite; a program needn't handle non-finite values.
Results may differ from the reference program's by a relative error of at most 0.012.
Values may be sent and summed in bfloat16 or wider, within the bound.
No kernel may reach another device: no remote copies, remote signals or barrier semaphores. Data moves between devices by JAX's collectives and lax.ppermute only.
A program may use at most 64 MiB of HBM per device.

```python
import math
import jax
import jax.numpy as jnp
from jax import lax

ROWS = 8192
RANK = 32
COLS = 2048
REPLICAS = 8


def draw_gradient(key, part):
    key = jax.random.fold_in(key, 7)
    key_col, key_row, key_noise = jax.random.split(key, 3)
    column_pos = jnp.arange(COLS, dtype=jnp.float32)
    col_scale = 10.0 ** (jax.random.uniform(key_col, (COLS,)) - 0.5) * (1.0 + 2.0 * column_pos / COLS)
    row_scale = 10.0 ** (jax.random.uniform(key_row, (ROWS,)) - 0.5)
    noise_draw = jax.random.normal(key_noise, (REPLICAS, COLS, ROWS))
    noise_draw = jnp.clip(noise_draw, -6.0, 6.0)
    return (3.0 * noise_draw * col_scale[None, :, None] * row_scale[None, None, :]).astype(jnp.bfloat16)


def block_scale(stream_key, shape, cuts, low, high):
    def one(dim, shards_of):
        steps = jax.random.uniform(jax.random.fold_in(jax.random.fold_in(stream_key, 6), dim), (shards_of,), jnp.float32, low / len(cuts), high / len(cuts))
        return jnp.repeat(jnp.exp(steps), shape[dim] // shards_of).reshape((-1,) + (1,) * (len(shape) - dim - 1))

    loudness = one(*cuts[0])
    for cut in cuts[1:]:
        loudness = loudness * one(*cut)
    return loudness


def normal_values(own_key, shape, scale, reach, cuts=(), kind=jnp.bfloat16):
    entries = scale * jax.random.normal(own_key, shape, jnp.float32)
    if cuts:
        entries = entries * block_scale(own_key, shape, cuts, -0.22, 0.18)
    return jnp.clip(entries, -reach, reach).astype(kind)


def setup_inputs(seed: int = 0) -> dict:
    keys = jax.random.split(jax.random.key(seed), 4)
    return {
        "gradient": draw_gradient(jax.random.fold_in(keys[3], 71), 0),
        "error_buffer": normal_values(keys[1], (REPLICAS, COLS, ROWS), 1.0, 6.0, ((0, 8), (1, 64))),
        "warm_factor": normal_values(keys[2], (RANK, COLS), 1.0, 6.0, ((1, 64),), jnp.float32),
    }


def merged_tile(grad_tile, error_tile):
    return (grad_tile.astype(jnp.float32) + error_tile.astype(jnp.float32)).astype(jnp.bfloat16)

def lower_factor(gram_matrix):
    rank_dim = gram_matrix.shape[0]
    ridge_term = 0.0001 * jnp.trace(gram_matrix) / rank_dim
    return jnp.linalg.cholesky(gram_matrix + ridge_term * jnp.eye(rank_dim, dtype=gram_matrix.dtype))

def reference(gradient, error_buffer, warm_factor):
    warm_bf = warm_factor.astype(jnp.bfloat16)

    def row_step(running, pair):
        tile = merged_tile(pair[0], pair[1])
        return (running + jnp.dot(warm_bf.astype(jnp.float32), tile.astype(jnp.float32), preferred_element_type=jnp.float32), None)
    running, _ = lax.scan(row_step, jnp.zeros((RANK, ROWS), jnp.float32), (gradient, error_buffer))
    row_factor = running / REPLICAS
    gram_matrix = jnp.dot(row_factor, row_factor.T, precision=lax.Precision.HIGHEST)
    lower = lower_factor(gram_matrix)
    basis = lax.linalg.triangular_solve(lower, row_factor, left_side=True, lower=True).astype(jnp.bfloat16)

    def col_step(running_q, pair):
        tile = merged_tile(pair[0], pair[1])
        term = lax.dot_general(basis.astype(jnp.float32), tile.astype(jnp.float32), (((1,), (1,)), ((), ())), preferred_element_type=jnp.float32)
        return (running_q + term, None)
    summed_q, _ = lax.scan(col_step, jnp.zeros((RANK, COLS), jnp.float32), (gradient, error_buffer))
    next_factor = summed_q / REPLICAS
    norm_sq = jnp.sum(next_factor * next_factor)
    norm_limit = 0.1 * math.sqrt(COLS * ROWS)
    clip_scale = jnp.minimum(1.0, norm_limit / jnp.sqrt(norm_sq + 1e-06))
    decompressed = lax.dot_general(next_factor.astype(jnp.bfloat16).astype(jnp.float32), basis.astype(jnp.float32), (((0,), (0,)), ((), ())), preferred_element_type=jnp.float32)
    applied_update = (clip_scale * decompressed).astype(jnp.bfloat16)

    def error_step(pair):
        tile = merged_tile(pair[0], pair[1])
        return (tile.astype(jnp.float32) - decompressed).astype(jnp.bfloat16)
    next_error = lax.map(error_step, (gradient, error_buffer))
    return (applied_update, next_error, next_factor)
```

```python
import math

import jax
import jax.numpy as jnp
from jax import lax
from jax.experimental import pallas as pl
from jax.experimental.pallas import tpu as pltpu
from jax.sharding import PartitionSpec as P

F32 = jnp.float32
BF16 = jnp.bfloat16
HIGHEST = lax.Precision.HIGHEST
PARAMS = pltpu.CompilerParams(vmem_limit_bytes=16 * 1024 * 1024)


def split3(value):
    high = value.astype(BF16)
    rest = value - high.astype(F32)
    middle = rest.astype(BF16)
    low = (rest - middle.astype(F32)).astype(BF16)
    return high, middle, low


def merge_kernel(gradient_ref, error_ref, warm_ref, send_ref):
    peers, half, _ = send_ref.shape
    chunk = gradient_ref.shape[1] // peers
    rank, width = warm_ref.shape
    warm = warm_ref[...].astype(BF16)
    packed = jnp.concatenate(
        [warm[:half], warm[half:], jnp.zeros((half, 128 - 2 * width), BF16)], axis=1
    )
    for peer in range(peers):
        part = slice(peer * chunk, (peer + 1) * chunk)
        tile = (gradient_ref[:, part].astype(F32) + error_ref[:, part].astype(F32)).astype(BF16)
        send_ref[peer, :, 0:chunk] = tile[:half]
        send_ref[peer, :, chunk : 2 * chunk] = tile[half:]
        send_ref[peer, :, 2 * chunk :] = packed


def rows_kernel(groups, width, scale, got_ref, mean_ref, send_ref):
    peers, half, wide = got_ref.shape
    chunk = (wide - 128) // 2
    replicas = peers // groups
    warm = []
    for group in range(groups):
        total = got_ref[group, :, 0 : 2 * chunk].astype(F32)
        for replica in range(1, replicas):
            total += got_ref[replica * groups + group, :, 0 : 2 * chunk].astype(F32)
        total *= scale
        top = group * 2 * half
        mean_ref[top : top + half, :] = total[:, :chunk]
        mean_ref[top + half : top + 2 * half, :] = total[:, chunk:]
        packed = got_ref[group, :, 2 * chunk :].astype(F32)
        warm.append(jnp.concatenate([packed[:, :width], packed[:, width : 2 * width]], axis=0))
    rows = jnp.dot(
        jnp.concatenate(warm, axis=1), mean_ref[...], precision=HIGHEST, preferred_element_type=F32
    ).astype(BF16)
    for peer in range(send_ref.shape[0]):
        send_ref[peer] = rows


def columns_kernel(groups, got_ref, mean_ref, send_ref):
    peers, rank, chunk = got_ref.shape
    total = got_ref[0].astype(F32)
    for peer in range(1, peers):
        total += got_ref[peer].astype(F32)
    rows = total.astype(BF16)
    product = lax.dot_general(
        rows.astype(F32),
        mean_ref[...],
        (((1,), (1,)), ((), ())),
        precision=HIGHEST,
        preferred_element_type=F32,
    )
    width = product.shape[1] // groups
    for group in range(groups):
        pieces = split3(product[:, group * width : (group + 1) * width])
        pad = jnp.zeros((rank, 128 - 3 * width), BF16)
        tail = jnp.concatenate([*pieces, pad], axis=1)
        for replica in range(send_ref.shape[0] // groups):
            send_ref[replica * groups + group, :, 0:chunk] = rows
            send_ref[replica * groups + group, :, chunk:] = tail


def factor_kernel(got_ref, rows_ref, next_ref, mix_ref, norm_ref):
    peers, rank, wide = got_ref.shape
    chunk = wide - 128
    width = next_ref.shape[1]
    tails = got_ref[0, :, chunk:].astype(F32)
    for peer in range(1, peers):
        tails += got_ref[peer, :, chunk:].astype(F32)
    product = tails[:, :width] + tails[:, width : 2 * width] + tails[:, 2 * width : 3 * width]
    for peer in range(peers):
        rows_ref[:, peer * chunk : (peer + 1) * chunk] = got_ref[peer, :, 0:chunk]
    rows = rows_ref[...]
    gram = lax.dot_general(rows, rows, (((1,), (1,)), ((), ())), preferred_element_type=F32)
    line = lax.broadcasted_iota(jnp.int32, (rank, rank), 0)
    eye = (line == lax.broadcasted_iota(jnp.int32, (rank, rank), 1)).astype(F32)
    trace = jnp.sum(gram * eye)
    gram = gram + (0.0001 * trace / rank) * eye
    work = jnp.concatenate([gram, product, eye], axis=1)
    line = lax.broadcasted_iota(jnp.int32, work.shape, 0)
    for step in range(rank):
        pivot_row = work[step : step + 1, :]
        scaled = pivot_row * lax.rsqrt(pivot_row[:, step : step + 1])
        column = work[:, step : step + 1] * lax.rsqrt(pivot_row[:, step : step + 1])
        work = jnp.where(line > step, work - column * scaled, jnp.where(line == step, scaled, work))
    next_factor = work[:, rank : rank + width]
    inverse = work[:, rank + width :]
    next_ref[...] = next_factor
    norm_ref[...] = jnp.full(norm_ref.shape, jnp.sum(next_factor * next_factor), F32)
    mix = lax.dot_general(
        next_factor,
        inverse,
        (((0,), (0,)), ((), ())),
        precision=HIGHEST,
        preferred_element_type=F32,
    )
    mix_ref[...] = jnp.concatenate([*split3(mix), jnp.zeros((width, 128 - 3 * rank), BF16)], axis=1)


def update_kernel(norm_limit, norms_ref, mix_ref, rows_ref, gradient_ref, error_ref, applied_ref, next_ref):
    rank, row_count = rows_ref.shape
    norm_sq = jnp.sum(norms_ref[...][:, 0:1])
    clip_scale = jnp.minimum(1.0, norm_limit * lax.rsqrt(jnp.full((1, 1), norm_sq + 1e-06, F32)))
    mix = mix_ref[...][:, : 3 * rank]
    step = 1024
    for start in range(0, row_count, step):
        part = slice(start, start + step)
        rows = rows_ref[:, part]
        decompressed = jnp.dot(
            mix, jnp.concatenate([rows, rows, rows], axis=0), preferred_element_type=F32
        )
        applied_ref[:, part] = (clip_scale * decompressed).astype(BF16)
        tile = (gradient_ref[:, part].astype(F32) + error_ref[:, part].astype(F32)).astype(BF16)
        next_ref[:, part] = (tile.astype(F32) - decompressed).astype(BF16)


def call(kernel, outs, *args):
    return pl.pallas_call(
        kernel,
        out_shape=outs,
        in_specs=[pl.BlockSpec(memory_space=pltpu.VMEM)] * len(args),
        out_specs=jax.tree.map(lambda _: pl.BlockSpec(memory_space=pltpu.VMEM), outs),
        compiler_params=PARAMS,
    )(*args)


def per_device(gradient, error_buffer, warm_factor):
    shape = jax.ShapeDtypeStruct
    replicas, depth, groups = (lax.axis_size(axis) for axis in ("gx", "gy", "gz"))
    gradient, error_buffer = gradient[0], error_buffer[0]
    width, row_count = gradient.shape
    rank = warm_factor.shape[0]
    peers = replicas * groups
    chunk = row_count // peers
    norm_limit = 0.1 * math.sqrt(width * depth * groups * row_count)

    send = call(
        merge_kernel, shape((peers, width // 2, 2 * chunk + 128), BF16), gradient, error_buffer, warm_factor
    )
    got = lax.all_to_all(send, ("gx", "gz"), 0, 0)
    mean, send = call(
        lambda *refs: rows_kernel(groups, width, 1.0 / replicas, *refs),
        (shape((groups * width, chunk), F32), shape((depth, rank, chunk), BF16)),
        got,
    )
    got = lax.all_to_all(send, "gy", 0, 0)
    send = call(
        lambda *refs: columns_kernel(groups, *refs), shape((peers, rank, chunk + 128), BF16), got, mean
    )
    got = lax.all_to_all(send, ("gx", "gz"), 0, 0)
    rows, next_factor, mix, norm = call(
        factor_kernel,
        (
            shape((rank, row_count), BF16),
            shape((rank, width), F32),
            shape((width, 128), BF16),
            shape((depth * groups, 128), F32),
        ),
        got,
    )
    norms = lax.all_to_all(norm, ("gy", "gz"), 0, 0, tiled=True)
    applied, next_error = call(
        lambda *refs: update_kernel(norm_limit, *refs),
        (shape((width, row_count), BF16), shape((width, row_count), BF16)),
        norms,
        mix,
        rows,
        gradient,
        error_buffer,
    )
    return applied, next_error[None], next_factor


def solution(mesh):
    in_specs = (P("gx", ("gy", "gz"), None), P("gx", ("gy", "gz"), None), P(None, ("gy", "gz")))
    out_specs = (P(("gy", "gz"), None), P("gx", ("gy", "gz"), None), P(None, ("gy", "gz")))
    return jax.shard_map(
        per_device, mesh=mesh, in_specs=in_specs, out_specs=out_specs, check_vma=False
    )
```

```python
import math

import jax
import jax.numpy as jnp
from jax import lax
from jax.experimental import pallas as pl
from jax.experimental.pallas import tpu as pltpu
from jax.sharding import PartitionSpec as P

F32 = jnp.float32
BF16 = jnp.bfloat16
HIGHEST = lax.Precision.HIGHEST
PARAMS = pltpu.CompilerParams(vmem_limit_bytes=16 * 1024 * 1024)


def split(value, pieces):
    parts = []
    for _ in range(pieces):
        part = value.astype(BF16)
        parts.append(part)
        value = value - part.astype(F32)
    return parts


def merge_kernel(gradient_ref, error_ref, warm_ref, send_ref, gradient_tile, error_tile, warm_tile, sems):
    peers, half, _ = send_ref.shape
    chunk = gradient_ref.shape[1] // peers
    rank, width = warm_ref.shape
    pieces = sems.shape[0]
    per_piece = peers // pieces
    copies = []
    for piece in range(pieces):
        part = pl.ds(piece * per_piece * chunk, per_piece * chunk)
        copies.append(
            (
                pltpu.make_async_copy(gradient_ref.at[:, part], gradient_tile.at[:, part], sems.at[piece, 0]),
                pltpu.make_async_copy(error_ref.at[:, part], error_tile.at[:, part], sems.at[piece, 1]),
            )
        )
    warm_copy = pltpu.make_async_copy(warm_ref, warm_tile, sems.at[0, 2])
    warm_copy.start()
    for pair in copies:
        pair[0].start()
        pair[1].start()
    warm_copy.wait()
    warm = warm_tile[...].astype(BF16)
    packed = jnp.concatenate(
        [warm[:half], warm[half:], jnp.zeros((half, 128 - 2 * width), BF16)], axis=1
    )
    for peer in range(peers):
        if peer % per_piece == 0:
            copies[peer // per_piece][0].wait()
            copies[peer // per_piece][1].wait()
        part = slice(peer * chunk, (peer + 1) * chunk)
        tile = (gradient_tile[:, part].astype(F32) + error_tile[:, part].astype(F32)).astype(BF16)
        send_ref[peer, :, 0:chunk] = tile[:half]
        send_ref[peer, :, chunk : 2 * chunk] = tile[half:]
        send_ref[peer, :, 2 * chunk :] = packed


def rows_kernel(groups, width, scale, got_ref, mean_ref, send_ref):
    peers, half, wide = got_ref.shape
    chunk = (wide - 128) // 2
    replicas = peers // groups
    warm = []
    for group in range(groups):
        total = got_ref[group, :, 0 : 2 * chunk].astype(F32)
        for replica in range(1, replicas):
            total += got_ref[replica * groups + group, :, 0 : 2 * chunk].astype(F32)
        total *= scale
        top = group * 2 * half
        mean_ref[top : top + half, :] = total[:, :chunk]
        mean_ref[top + half : top + 2 * half, :] = total[:, chunk:]
        packed = got_ref[group, :, 2 * chunk :].astype(F32)
        warm.append(jnp.concatenate([packed[:, :width], packed[:, width : 2 * width]], axis=0))
    rows = jnp.dot(
        jnp.concatenate(warm, axis=1), mean_ref[...], precision=HIGHEST, preferred_element_type=F32
    ).astype(BF16)
    for peer in range(send_ref.shape[0]):
        send_ref[peer] = rows


def add(got_ref):
    total = got_ref[0].astype(F32)
    for peer in range(1, got_ref.shape[0]):
        total += got_ref[peer].astype(F32)
    return total.astype(BF16)


def sum_kernel(got_ref, send_ref):
    total = add(got_ref)
    for peer in range(send_ref.shape[0]):
        send_ref[peer] = total


def columns_kernel(groups, got_ref, mean_ref, send_ref):
    chunk = got_ref.shape[2]
    half = send_ref.shape[1]
    rows = add(got_ref)
    product = lax.dot_general(
        rows.astype(F32),
        mean_ref[...],
        (((1,), (1,)), ((), ())),
        precision=HIGHEST,
        preferred_element_type=F32,
    )
    width = product.shape[1] // groups
    for group in range(groups):
        high, low = split(product[:, group * width : (group + 1) * width], 2)
        tail = jnp.concatenate([high[:half], high[half:], low[:half], low[half:]], axis=1)
        for replica in range(send_ref.shape[0] // groups):
            peer = replica * groups + group
            send_ref[peer, :, 0:chunk] = rows[:half]
            send_ref[peer, :, chunk : 2 * chunk] = rows[half:]
            send_ref[peer, :, 2 * chunk :] = tail


def factor_kernel(got_ref, rows_ref, next_ref, mix_ref, norm_ref):
    peers, half, wide = got_ref.shape
    chunk = (wide - 128) // 2
    rank, width = next_ref.shape
    tails = got_ref[0, :, 2 * chunk :].astype(F32)
    for peer in range(1, peers):
        tails += got_ref[peer, :, 2 * chunk :].astype(F32)
    tails = tails[:, : 2 * width] + tails[:, 2 * width :]
    product = jnp.concatenate([tails[:, :width], tails[:, width:]], axis=0)
    for peer in range(peers):
        part = slice(peer * chunk, (peer + 1) * chunk)
        rows_ref[0:half, part] = got_ref[peer, :, 0:chunk]
        rows_ref[half:rank, part] = got_ref[peer, :, chunk : 2 * chunk]
    rows = rows_ref[...]
    gram = lax.dot_general(rows, rows, (((1,), (1,)), ((), ())), preferred_element_type=F32)
    line = lax.broadcasted_iota(jnp.int32, (rank, rank), 0)
    eye = (line == lax.broadcasted_iota(jnp.int32, (rank, rank), 1)).astype(F32)
    trace = jnp.sum(gram * eye)
    gram = gram + (0.0001 * trace / rank) * eye
    work = jnp.concatenate([gram, product, eye], axis=1)
    line = lax.broadcasted_iota(jnp.int32, work.shape, 0)
    for step in range(rank):
        pivot_row = work[step : step + 1, :]
        scaled = pivot_row * lax.rsqrt(pivot_row[:, step : step + 1])
        column = work[:, step : step + 1] * lax.rsqrt(pivot_row[:, step : step + 1])
        work = jnp.where(line > step, work - column * scaled, jnp.where(line == step, scaled, work))
    next_factor = work[:, rank : rank + width]
    inverse = work[:, rank + width :]
    next_ref[...] = next_factor
    norm_ref[...] = jnp.full(norm_ref.shape, jnp.sum(next_factor * next_factor), F32)
    mix = lax.dot_general(
        next_factor,
        inverse,
        (((0,), (0,)), ((), ())),
        precision=HIGHEST,
        preferred_element_type=F32,
    )
    mix_ref[...] = jnp.concatenate([*split(mix, 3), jnp.zeros((width, 128 - 3 * rank), BF16)], axis=1)


def update_kernel(norm_limit, norms_ref, mix_ref, rows_ref, gradient_ref, error_ref, applied_ref, next_ref):
    rank, row_count = rows_ref.shape
    norm_sq = jnp.sum(norms_ref[...][:, 0:1])
    clip_scale = jnp.minimum(1.0, norm_limit * lax.rsqrt(jnp.full((1, 1), norm_sq + 1e-06, F32)))
    mix = mix_ref[...][:, : 3 * rank]
    step = 1024
    for start in range(0, row_count, step):
        part = slice(start, start + step)
        rows = rows_ref[:, part]
        decompressed = jnp.dot(
            mix, jnp.concatenate([rows, rows, rows], axis=0), preferred_element_type=F32
        )
        applied_ref[:, part] = (clip_scale * decompressed).astype(BF16)
        tile = (gradient_ref[:, part].astype(F32) + error_ref[:, part].astype(F32)).astype(BF16)
        next_ref[:, part] = (tile.astype(F32) - decompressed).astype(BF16)


def call(kernel, outs, *args, space=pltpu.VMEM, scratch=()):
    return pl.pallas_call(
        kernel,
        out_shape=outs,
        in_specs=[pl.BlockSpec(memory_space=space)] * len(args),
        out_specs=jax.tree.map(lambda _: pl.BlockSpec(memory_space=pltpu.VMEM), outs),
        scratch_shapes=scratch,
        compiler_params=PARAMS,
    )(*args)


def per_device(gradient, error_buffer, warm_factor):
    shape = jax.ShapeDtypeStruct
    replicas, far, near, groups = (lax.axis_size(axis) for axis in ("gx", "far", "near", "gz"))
    depth = far * near
    gradient, error_buffer = gradient[0], error_buffer[0]
    width, row_count = gradient.shape
    rank = warm_factor.shape[0]
    peers = replicas * groups
    chunk = row_count // peers
    norm_limit = 0.1 * math.sqrt(width * depth * groups * row_count)

    send = call(
        merge_kernel,
        shape((peers, width // 2, 2 * chunk + 128), BF16),
        gradient,
        error_buffer,
        warm_factor,
        space=pl.ANY,
        scratch=[
            pltpu.VMEM((width, row_count), BF16),
            pltpu.VMEM((width, row_count), BF16),
            pltpu.VMEM((rank, width), F32),
            pltpu.SemaphoreType.DMA((min(8, peers), 3)),
        ],
    )
    got = lax.all_to_all(send, ("gx", "gz"), 0, 0)
    mean, send = call(
        lambda *refs: rows_kernel(groups, width, 1.0 / replicas, *refs),
        (shape((groups * width, chunk), F32), shape((far, rank, chunk), BF16)),
        got,
    )
    got = lax.all_to_all(send, "far", 0, 0)
    send = call(sum_kernel, shape((near, rank, chunk), BF16), got)
    got = lax.all_to_all(send, "near", 0, 0)
    send = call(
        lambda *refs: columns_kernel(groups, *refs),
        shape((peers, rank // 2, 2 * chunk + 128), BF16),
        got,
        mean,
    )
    got = lax.all_to_all(send, ("gx", "gz"), 0, 0)
    rows, next_factor, mix, norm = call(
        factor_kernel,
        (
            shape((rank, row_count), BF16),
            shape((rank, width), F32),
            shape((width, 128), BF16),
            shape((depth * groups, 128), F32),
        ),
        got,
    )
    norms = lax.all_to_all(norm, ("far", "near", "gz"), 0, 0, tiled=True)
    applied, next_error = call(
        lambda *refs: update_kernel(norm_limit, *refs),
        (shape((width, row_count), BF16), shape((width, row_count), BF16)),
        norms,
        mix,
        rows,
        gradient,
        error_buffer,
    )
    return applied, next_error[None], next_factor


def solution(mesh):
    replicas, depth, groups = (mesh.shape[axis] for axis in ("gx", "gy", "gz"))
    near = max(n for n in range(1, depth + 1) if depth % n == 0 and n * n <= depth)
    fine = jax.sharding.Mesh(
        mesh.devices.reshape(replicas, depth // near, near, groups), ("gx", "far", "near", "gz")
    )
    columns = ("far", "near", "gz")
    in_specs = (P("gx", columns, None), P("gx", columns, None), P(None, columns))
    out_specs = (P(columns, None), P("gx", columns, None), P(None, columns))
    return jax.shard_map(
        per_device, mesh=fine, in_specs=in_specs, out_specs=out_specs, check_vma=False
    )
```

```python
import math

import jax
import jax.numpy as jnp
from jax import lax
from jax.experimental import pallas as pl
from jax.experimental.pallas import tpu as pltpu
from jax.sharding import PartitionSpec as P

F32 = jnp.float32
BF16 = jnp.bfloat16
HIGHEST = lax.Precision.HIGHEST
LANES = 128


def split(value, pieces):
    parts = []
    for _ in range(pieces):
        part = value.astype(BF16)
        parts.append(part)
        value = value - part.astype(F32)
    return parts


def merge_kernel(
    gradient_ref, error_ref, warm_ref, send_ref, gradient_tile, error_tile, warm_tile, send_tile, got_sems, put_sems
):
    peers, tall, _ = send_ref.shape
    width, row_count = gradient_ref.shape
    chunk = row_count // peers
    rank = warm_ref.shape[0]
    pieces = put_sems.shape[0]
    per_piece = peers // pieces
    gets, puts = [], []
    for piece in range(pieces):
        part = pl.ds(piece * per_piece * chunk, per_piece * chunk)
        mine = pl.ds(piece * per_piece, per_piece)
        gets.append(
            (
                pltpu.make_async_copy(gradient_ref.at[:, part], gradient_tile.at[:, part], got_sems.at[piece, 0]),
                pltpu.make_async_copy(error_ref.at[:, part], error_tile.at[:, part], got_sems.at[piece, 1]),
            )
        )
        puts.append(pltpu.make_async_copy(send_tile.at[mine], send_ref.at[mine], put_sems.at[piece]))
    warm_get = pltpu.make_async_copy(warm_ref, warm_tile, got_sems.at[0, 2])
    warm_get.start()
    for pair in gets:
        pair[0].start()
        pair[1].start()
    warm_get.wait()
    half = rank // 2
    packed = jnp.concatenate(
        [warm_tile[:half], warm_tile[half:], jnp.zeros((half, LANES - 2 * width), F32)], axis=1
    ).astype(BF16)
    for piece in range(pieces):
        gets[piece][0].wait()
        gets[piece][1].wait()
        for peer in range(piece * per_piece, (piece + 1) * per_piece):
            for i in range(chunk // LANES):
                part = slice(peer * chunk + i * LANES, peer * chunk + (i + 1) * LANES)
                tile = gradient_tile[:, part].astype(F32) + error_tile[:, part].astype(F32)
                send_tile[peer, i * width : (i + 1) * width, :] = tile.astype(BF16)
            send_tile[peer, tall - half :, :] = packed
        puts[piece].start()
    for put in puts:
        put.wait()


def rows_kernel(groups, width, scale, got_ref, mean_ref, send_ref):
    peers, tall, _ = got_ref.shape
    chunk = mean_ref.shape[1]
    high = width * chunk // LANES
    replicas = peers // groups
    warm = []
    for group in range(groups):
        total = got_ref[group, 0:high, :].astype(F32)
        for replica in range(1, replicas):
            total += got_ref[replica * groups + group, 0:high, :].astype(F32)
        total *= scale
        for i in range(chunk // LANES):
            mean_ref[group * width : (group + 1) * width, i * LANES : (i + 1) * LANES] = total[
                i * width : (i + 1) * width
            ]
        packed = got_ref[group, high:, :].astype(F32)
        warm.append(jnp.concatenate([packed[:, :width], packed[:, width : 2 * width]], axis=0))
    rows = jnp.dot(
        jnp.concatenate(warm, axis=1), mean_ref[...], precision=HIGHEST, preferred_element_type=F32
    ).astype(BF16)
    for peer in range(send_ref.shape[0]):
        send_ref[peer] = rows


def add(got_ref):
    total = got_ref[0].astype(F32)
    for peer in range(1, got_ref.shape[0]):
        total += got_ref[peer].astype(F32)
    return total.astype(BF16)


def sum_kernel(got_ref, send_ref):
    total = add(got_ref)
    for peer in range(send_ref.shape[0]):
        send_ref[peer] = total


def columns_kernel(groups, got_ref, mean_ref, send_ref):
    rank, chunk = got_ref.shape[1:]
    half = rank // 2
    rows = add(got_ref)
    product = lax.dot_general(
        rows.astype(F32),
        mean_ref[...],
        (((1,), (1,)), ((), ())),
        precision=HIGHEST,
        preferred_element_type=F32,
    )
    width = product.shape[1] // groups
    for group in range(groups):
        high, low = split(product[:, group * width : (group + 1) * width], 2)
        tail = jnp.concatenate([high[:half], high[half:], low[:half], low[half:]], axis=1)
        for replica in range(send_ref.shape[0] // groups):
            peer = replica * groups + group
            for i in range(chunk // LANES):
                send_ref[peer, i * rank : (i + 1) * rank, :] = rows[:, i * LANES : (i + 1) * LANES]
            send_ref[peer, chunk // LANES * rank :, :] = tail


def eliminate(gram, product):
    rank, width = product.shape
    columns = [
        jnp.broadcast_to(gram[8 * (j // 8) :, j : j + 1], (rank - 8 * (j // 8), LANES))
        for j in range(rank)
    ]
    line = lax.broadcasted_iota(jnp.int32, (rank, LANES), 0)
    lane = lax.broadcasted_iota(jnp.int32, (rank, LANES), 1)
    work = jnp.concatenate([product, jnp.zeros((rank, LANES - width), F32)], axis=1)
    work = jnp.where(lane == line + width, 1.0, work)
    for k in range(rank):
        top = 8 * (k // 8)
        column = columns[k]
        inverse_root = lax.rsqrt(column[k - top : k - top + 1])
        column = column * inverse_root
        for j in range(k + 1, rank):
            first = 8 * (j // 8) - top
            columns[j] = columns[j] - column[first:] * column[j - top : j - top + 1]
        row = work[k : k + 1] * inverse_root
        rest = work[top:] - jnp.where(line[top:] > k, column, 0.0) * row
        rest = jnp.where(line[top:] == k, row, rest)
        work = jnp.concatenate([work[:top], rest], axis=0) if top else rest
    return work[:, width : width + rank], work[:, :width]


def factor_kernel(got_ref, next_ref, mix_ref, norm_ref):
    peers, tall, _ = got_ref.shape
    rank, width = next_ref.shape
    high = tall - rank // 2
    tails = got_ref[0, high:, :].astype(F32)
    for peer in range(1, peers):
        tails += got_ref[peer, high:, :].astype(F32)
    tails = tails[:, : 2 * width] + tails[:, 2 * width :]
    product = jnp.concatenate([tails[:, :width], tails[:, width:]], axis=0)
    gram = jnp.zeros((rank, rank), F32)
    for peer in range(peers):
        rows = jnp.concatenate(
            [got_ref[peer, i : i + rank, :] for i in range(0, high, rank)], axis=1
        )
        gram += lax.dot_general(rows, rows, (((1,), (1,)), ((), ())), preferred_element_type=F32)
    line = lax.broadcasted_iota(jnp.int32, (rank, rank), 0)
    eye = (line == lax.broadcasted_iota(jnp.int32, (rank, rank), 1)).astype(F32)
    trace = jnp.sum(gram * eye)
    inverse, next_factor = eliminate(gram + (0.0001 * trace / rank) * eye, product)
    next_ref[...] = next_factor
    norm_ref[...] = jnp.full(norm_ref.shape, jnp.sum(next_factor * next_factor), F32)
    mix = lax.dot_general(
        next_factor,
        inverse,
        (((0,), (0,)), ((), ())),
        precision=HIGHEST,
        preferred_element_type=F32,
    )
    mix_ref[...] = jnp.concatenate(
        [*split(mix, 3), jnp.zeros((width, LANES - 3 * rank), BF16)], axis=1
    )


def residual_kernel(got_ref, mix_ref, gradient_ref, error_ref, decompressed_ref, next_ref):
    peers, tall, _ = got_ref.shape
    rank = next_ref.shape[0]
    high = tall - rank // 2
    chunk = high // rank * LANES
    mix = mix_ref[...][:, : 3 * rank]
    for peer in range(peers):
        part = slice(peer * chunk, (peer + 1) * chunk)
        rows = jnp.concatenate(
            [got_ref[peer, i : i + rank, :] for i in range(0, high, rank)], axis=1
        )
        decompressed = jnp.dot(
            mix, jnp.concatenate([rows, rows, rows], axis=0), preferred_element_type=F32
        )
        decompressed_ref[:, part] = decompressed
        tile = (gradient_ref[:, part].astype(F32) + error_ref[:, part].astype(F32)).astype(BF16)
        next_ref[:, part] = (tile.astype(F32) - decompressed).astype(BF16)


def clip_kernel(norm_limit, norms_ref, decompressed_ref, applied_ref, tile, sems):
    norm_sq = jnp.sum(norms_ref[...][:, 0:1])
    clip_scale = jnp.minimum(1.0, norm_limit * lax.rsqrt(jnp.full((1, 1), norm_sq + 1e-06, F32)))
    pieces = sems.shape[0]
    step = applied_ref.shape[1] // pieces
    puts = []
    for piece in range(pieces):
        part = pl.ds(piece * step, step)
        tile[:, part] = (clip_scale * decompressed_ref[:, part]).astype(BF16)
        put = pltpu.make_async_copy(tile.at[:, part], applied_ref.at[:, part], sems.at[piece])
        put.start()
        puts.append(put)
    for put in puts:
        put.wait()


def call(kernel, outs, *args, vmem=16, spaces=None, out_space=pltpu.VMEM, scratch=(), cost=None):
    spaces = spaces or [pltpu.VMEM] * len(args)
    return pl.pallas_call(
        kernel,
        out_shape=outs,
        in_specs=[pl.BlockSpec(memory_space=space) for space in spaces],
        out_specs=jax.tree.map(lambda _: pl.BlockSpec(memory_space=out_space), outs),
        scratch_shapes=scratch,
        compiler_params=pltpu.CompilerParams(vmem_limit_bytes=vmem * 1024 * 1024),
        cost_estimate=cost,
    )(*args)


def per_device(gradient, error_buffer, warm_factor):
    shape = jax.ShapeDtypeStruct
    replicas, far, near, groups = (lax.axis_size(axis) for axis in ("gx", "far", "near", "gz"))
    plane, columns = ("gx", "gz"), far * near * groups
    gradient, error_buffer = gradient[0], error_buffer[0]
    width, row_count = gradient.shape
    rank = warm_factor.shape[0]
    peers = replicas * groups
    chunk = row_count // peers
    norm_limit = 0.1 * math.sqrt(width * columns * row_count)
    pieces = min(8, peers)
    message = shape((peers, width * chunk // LANES + rank // 2, LANES), BF16)

    send = call(
        merge_kernel,
        message,
        gradient,
        error_buffer,
        warm_factor,
        vmem=60,
        spaces=[pl.ANY] * 3,
        out_space=pl.ANY,
        scratch=[
            pltpu.VMEM((width, row_count), BF16),
            pltpu.VMEM((width, row_count), BF16),
            pltpu.VMEM((rank, width), F32),
            pltpu.VMEM(message.shape, BF16),
            pltpu.SemaphoreType.DMA((pieces, 3)),
            pltpu.SemaphoreType.DMA((pieces,)),
        ],
    )
    got = lax.all_to_all(send, plane, 0, 0)
    mean, send = call(
        lambda *refs: rows_kernel(groups, width, 1.0 / replicas, *refs),
        (shape((groups * width, chunk), F32), shape((far, rank, chunk), BF16)),
        got,
    )
    got = lax.all_to_all(send, "far", 0, 0)
    send = call(sum_kernel, shape((near, rank, chunk), BF16), got)
    got = lax.all_to_all(send, "near", 0, 0)
    message = shape((peers, rank * chunk // LANES + rank // 2, LANES), BF16)
    send = call(lambda *refs: columns_kernel(groups, *refs), message, got, mean)
    got = lax.all_to_all(send, plane, 0, 0)
    next_factor, mix, norm = call(
        factor_kernel,
        (shape((rank, width), F32), shape((width, LANES), BF16), shape((columns, LANES), F32)),
        got,
    )
    norms = lax.all_to_all(norm, ("far", "near", "gz"), 0, 0, tiled=True)
    decompressed, next_error = call(
        residual_kernel,
        (shape((width, row_count), F32), shape((width, row_count), BF16)),
        got,
        mix,
        gradient,
        error_buffer,
        cost=pl.CostEstimate(
            flops=6 * rank * width * row_count, bytes_accessed=10 * width * row_count, transcendentals=0
        ),
    )
    applied = call(
        lambda *refs: clip_kernel(norm_limit, *refs),
        shape((width, row_count), BF16),
        norms,
        decompressed,
        out_space=pl.ANY,
        scratch=[pltpu.VMEM((width, row_count), BF16), pltpu.SemaphoreType.DMA((8,))],
    )
    return applied, next_error[None], next_factor


def solution(mesh):
    replicas, depth, groups = (mesh.shape[axis] for axis in ("gx", "gy", "gz"))
    near = max(n for n in range(1, depth + 1) if depth % n == 0 and n * n <= depth)
    fine = jax.sharding.Mesh(
        mesh.devices.reshape(replicas, depth // near, near, groups), ("gx", "far", "near", "gz")
    )
    columns = ("far", "near", "gz")
    in_specs = (P("gx", columns, None), P("gx", columns, None), P(None, columns))
    out_specs = (P(columns, None), P("gx", columns, None), P(None, columns))
    return jax.shard_map(
        per_device, mesh=fine, in_specs=in_specs, out_specs=out_specs, check_vma=False
    )
```

```python
import math

import jax
import jax.numpy as jnp
from jax import lax
from jax.experimental import pallas as pl
from jax.experimental.pallas import tpu as pltpu
from jax.sharding import PartitionSpec as P

F32 = jnp.float32
BF16 = jnp.bfloat16
HIGHEST = lax.Precision.HIGHEST
LANES = 128


def split(value, pieces):
    parts = []
    for _ in range(pieces):
        part = value.astype(BF16)
        parts.append(part)
        value = value - part.astype(F32)
    return parts


def merge_kernel(
    gradient_ref, error_ref, warm_ref, send_ref, gradient_tile, error_tile, warm_tile, send_tile, got_sems, put_sems
):
    peers, tall, _ = send_ref.shape
    width, row_count = gradient_ref.shape
    chunk = row_count // peers
    rank = warm_ref.shape[0]
    pieces = put_sems.shape[0]
    per_piece = peers // pieces
    gets, puts = [], []
    for piece in range(pieces):
        part = pl.ds(piece * per_piece * chunk, per_piece * chunk)
        mine = pl.ds(piece * per_piece, per_piece)
        gets.append(
            (
                pltpu.make_async_copy(gradient_ref.at[:, part], gradient_tile.at[:, part], got_sems.at[piece, 0]),
                pltpu.make_async_copy(error_ref.at[:, part], error_tile.at[:, part], got_sems.at[piece, 1]),
            )
        )
        puts.append(pltpu.make_async_copy(send_tile.at[mine], send_ref.at[mine], put_sems.at[piece]))
    warm_get = pltpu.make_async_copy(warm_ref, warm_tile, got_sems.at[0, 2])
    warm_get.start()
    for pair in gets:
        pair[0].start()
        pair[1].start()
    warm_get.wait()
    half = rank // 2
    packed = jnp.concatenate(
        [warm_tile[:half], warm_tile[half:], jnp.zeros((half, LANES - 2 * width), F32)], axis=1
    ).astype(BF16)
    for piece in range(pieces):
        gets[piece][0].wait()
        gets[piece][1].wait()
        for peer in range(piece * per_piece, (piece + 1) * per_piece):
            for i in range(chunk // LANES):
                part = slice(peer * chunk + i * LANES, peer * chunk + (i + 1) * LANES)
                tile = gradient_tile[:, part].astype(F32) + error_tile[:, part].astype(F32)
                send_tile[peer, i * width : (i + 1) * width, :] = tile.astype(BF16)
            send_tile[peer, tall - half :, :] = packed
        puts[piece].start()
    for put in puts:
        put.wait()


def rows_kernel(groups, width, scale, got_ref, mean_ref, send_ref):
    peers, tall, _ = got_ref.shape
    chunk = mean_ref.shape[1]
    high = width * chunk // LANES
    replicas = peers // groups
    warm = []
    for group in range(groups):
        total = got_ref[group, 0:high, :].astype(F32)
        for replica in range(1, replicas):
            total += got_ref[replica * groups + group, 0:high, :].astype(F32)
        total *= scale
        for i in range(chunk // LANES):
            mean_ref[group * width : (group + 1) * width, i * LANES : (i + 1) * LANES] = total[
                i * width : (i + 1) * width
            ]
        packed = got_ref[group, high:, :].astype(F32)
        warm.append(jnp.concatenate([packed[:, :width], packed[:, width : 2 * width]], axis=0))
    rows = jnp.dot(
        jnp.concatenate(warm, axis=1), mean_ref[...], precision=HIGHEST, preferred_element_type=F32
    ).astype(BF16)
    for peer in range(send_ref.shape[0]):
        send_ref[peer] = rows


def add(got_ref):
    total = got_ref[0].astype(F32)
    for peer in range(1, got_ref.shape[0]):
        total += got_ref[peer].astype(F32)
    return total.astype(BF16)


def columns_kernel(groups, got_ref, mean_ref, send_ref):
    rank, chunk = got_ref.shape[1:]
    half = rank // 2
    rows = add(got_ref)
    product = lax.dot_general(
        rows.astype(F32),
        mean_ref[...],
        (((1,), (1,)), ((), ())),
        precision=HIGHEST,
        preferred_element_type=F32,
    )
    width = product.shape[1] // groups
    for group in range(groups):
        high, low = split(product[:, group * width : (group + 1) * width], 2)
        tail = jnp.concatenate([high[:half], high[half:], low[:half], low[half:]], axis=1)
        for replica in range(send_ref.shape[0] // groups):
            peer = replica * groups + group
            for i in range(chunk // LANES):
                send_ref[peer, i * rank : (i + 1) * rank, :] = rows[:, i * LANES : (i + 1) * LANES]
            send_ref[peer, chunk // LANES * rank :, :] = tail


def eliminate(gram, product):
    rank, width = product.shape
    columns = [
        jnp.broadcast_to(gram[8 * (j // 8) :, j : j + 1], (rank - 8 * (j // 8), LANES))
        for j in range(rank)
    ]
    line = lax.broadcasted_iota(jnp.int32, (rank, LANES), 0)
    lane = lax.broadcasted_iota(jnp.int32, (rank, LANES), 1)
    work = jnp.concatenate([product, jnp.zeros((rank, LANES - width), F32)], axis=1)
    work = jnp.where(lane == line + width, 1.0, work)
    for k in range(rank):
        top = 8 * (k // 8)
        column = columns[k]
        inverse_root = lax.rsqrt(column[k - top : k - top + 1])
        column = column * inverse_root
        for j in range(k + 1, rank):
            first = 8 * (j // 8) - top
            columns[j] = columns[j] - column[first:] * column[j - top : j - top + 1]
        row = work[k : k + 1] * inverse_root
        rest = work[top:] - jnp.where(line[top:] > k, column, 0.0) * row
        rest = jnp.where(line[top:] == k, row, rest)
        work = jnp.concatenate([work[:top], rest], axis=0) if top else rest
    return work[:, width : width + rank], work[:, :width]


def factor_kernel(got_ref, next_ref, mix_ref, norm_ref):
    peers, tall, _ = got_ref.shape
    rank, width = next_ref.shape
    high = tall - rank // 2
    tails = got_ref[0, high:, :].astype(F32)
    for peer in range(1, peers):
        tails += got_ref[peer, high:, :].astype(F32)
    tails = tails[:, : 2 * width] + tails[:, 2 * width :]
    product = jnp.concatenate([tails[:, :width], tails[:, width:]], axis=0)
    gram = jnp.zeros((rank, rank), F32)
    for peer in range(peers):
        rows = jnp.concatenate(
            [got_ref[peer, i : i + rank, :] for i in range(0, high, rank)], axis=1
        )
        gram += lax.dot_general(rows, rows, (((1,), (1,)), ((), ())), preferred_element_type=F32)
    line = lax.broadcasted_iota(jnp.int32, (rank, rank), 0)
    eye = (line == lax.broadcasted_iota(jnp.int32, (rank, rank), 1)).astype(F32)
    trace = jnp.sum(gram * eye)
    inverse, next_factor = eliminate(gram + (0.0001 * trace / rank) * eye, product)
    next_ref[...] = next_factor
    norm_ref[...] = jnp.full(norm_ref.shape, jnp.sum(next_factor * next_factor), F32)
    mix = lax.dot_general(
        next_factor,
        inverse,
        (((0,), (0,)), ((), ())),
        precision=HIGHEST,
        preferred_element_type=F32,
    )
    mix_ref[...] = jnp.concatenate(
        [*split(mix, 3), jnp.zeros((width, LANES - 3 * rank), BF16)], axis=1
    )


def residual_kernel(got_ref, mix_ref, gradient_ref, error_ref, decompressed_ref, next_ref):
    peers, tall, _ = got_ref.shape
    rank = next_ref.shape[0]
    high = tall - rank // 2
    chunk = high // rank * LANES
    mix = mix_ref[...][:, : 3 * rank]
    for peer in range(peers):
        part = slice(peer * chunk, (peer + 1) * chunk)
        rows = jnp.concatenate(
            [got_ref[peer, i : i + rank, :] for i in range(0, high, rank)], axis=1
        )
        decompressed = jnp.dot(
            mix, jnp.concatenate([rows, rows, rows], axis=0), preferred_element_type=F32
        )
        decompressed_ref[:, part] = decompressed
        tile = (gradient_ref[:, part].astype(F32) + error_ref[:, part].astype(F32)).astype(BF16)
        next_ref[:, part] = (tile.astype(F32) - decompressed).astype(BF16)


def clip_kernel(norm_limit, norms_ref, decompressed_ref, applied_ref, tile, sems):
    norm_sq = jnp.sum(norms_ref[...][:, 0:1])
    clip_scale = jnp.minimum(1.0, norm_limit * lax.rsqrt(jnp.full((1, 1), norm_sq + 1e-06, F32)))
    pieces = sems.shape[0]
    step = applied_ref.shape[1] // pieces
    puts = []
    for piece in range(pieces):
        part = pl.ds(piece * step, step)
        tile[:, part] = (clip_scale * decompressed_ref[:, part]).astype(BF16)
        put = pltpu.make_async_copy(tile.at[:, part], applied_ref.at[:, part], sems.at[piece])
        put.start()
        puts.append(put)
    for put in puts:
        put.wait()


def call(kernel, outs, *args, vmem=16, spaces=None, out_space=pltpu.VMEM, scratch=(), cost=None):
    spaces = spaces or [pltpu.VMEM] * len(args)
    return pl.pallas_call(
        kernel,
        out_shape=outs,
        in_specs=[pl.BlockSpec(memory_space=space) for space in spaces],
        out_specs=jax.tree.map(lambda _: pl.BlockSpec(memory_space=out_space), outs),
        scratch_shapes=scratch,
        compiler_params=pltpu.CompilerParams(vmem_limit_bytes=vmem * 1024 * 1024),
        cost_estimate=cost,
    )(*args)


def per_device(gradient, error_buffer, warm_factor):
    shape = jax.ShapeDtypeStruct
    replicas, far, near, groups = (lax.axis_size(axis) for axis in ("gx", "far", "near", "gz"))
    plane, groups, columns = ("gx", "near", "gz"), near * groups, far * near * groups
    gradient, error_buffer = gradient[0], error_buffer[0]
    width, row_count = gradient.shape
    rank = warm_factor.shape[0]
    peers = replicas * groups
    chunk = row_count // peers
    norm_limit = 0.1 * math.sqrt(width * columns * row_count)
    pieces = min(8, peers)
    message = shape((peers, width * chunk // LANES + rank // 2, LANES), BF16)

    send = call(
        merge_kernel,
        message,
        gradient,
        error_buffer,
        warm_factor,
        vmem=60,
        spaces=[pl.ANY] * 3,
        out_space=pl.ANY,
        scratch=[
            pltpu.VMEM((width, row_count), BF16),
            pltpu.VMEM((width, row_count), BF16),
            pltpu.VMEM((rank, width), F32),
            pltpu.VMEM(message.shape, BF16),
            pltpu.SemaphoreType.DMA((pieces, 3)),
            pltpu.SemaphoreType.DMA((pieces,)),
        ],
    )
    got = lax.all_to_all(send, plane, 0, 0)
    mean, send = call(
        lambda *refs: rows_kernel(groups, width, 1.0 / replicas, *refs),
        (shape((groups * width, chunk), F32), shape((far, rank, chunk), BF16)),
        got,
    )
    got = lax.all_to_all(send, "far", 0, 0)
    message = shape((peers, rank * chunk // LANES + rank // 2, LANES), BF16)
    send = call(lambda *refs: columns_kernel(groups, *refs), message, got, mean)
    got = lax.all_to_all(send, plane, 0, 0)
    next_factor, mix, norm = call(
        factor_kernel,
        (shape((rank, width), F32), shape((width, LANES), BF16), shape((columns, LANES), F32)),
        got,
    )
    norms = lax.all_to_all(norm, ("far", "near", "gz"), 0, 0, tiled=True)
    decompressed, next_error = call(
        residual_kernel,
        (shape((width, row_count), F32), shape((width, row_count), BF16)),
        got,
        mix,
        gradient,
        error_buffer,
        cost=pl.CostEstimate(
            flops=6 * rank * width * row_count, bytes_accessed=10 * width * row_count, transcendentals=0
        ),
    )
    applied = call(
        lambda *refs: clip_kernel(norm_limit, *refs),
        shape((width, row_count), BF16),
        norms,
        decompressed,
        out_space=pl.ANY,
        scratch=[pltpu.VMEM((width, row_count), BF16), pltpu.SemaphoreType.DMA((8,))],
    )
    return applied, next_error[None], next_factor


def solution(mesh):
    replicas, depth, groups = (mesh.shape[axis] for axis in ("gx", "gy", "gz"))
    near = math.gcd(depth, 2)
    fine = jax.sharding.Mesh(
        mesh.devices.reshape(replicas, depth // near, near, groups), ("gx", "far", "near", "gz")
    )
    columns = ("far", "near", "gz")
    in_specs = (P("gx", columns, None), P("gx", columns, None), P(None, columns))
    out_specs = (P(columns, None), P("gx", columns, None), P(None, columns))
    return jax.shard_map(
        per_device, mesh=fine, in_specs=in_specs, out_specs=out_specs, check_vma=False
    )
```

```python
import math

import jax
import jax.numpy as jnp
from jax import lax
from jax.experimental import pallas as pl
from jax.experimental.pallas import tpu as pltpu
from jax.sharding import PartitionSpec as P

F32 = jnp.float32
BF16 = jnp.bfloat16
HIGHEST = lax.Precision.HIGHEST
LANES = 128


def split(value, pieces):
    parts = []
    for _ in range(pieces):
        part = value.astype(BF16)
        parts.append(part)
        value = value - part.astype(F32)
    return parts


def merge_kernel(gradient_ref, error_ref, warm_ref, send_ref, gradient_tile, error_tile, warm_tile, sems):
    peers, tall, _ = send_ref.shape
    width, row_count = gradient_ref.shape
    chunk = row_count // peers
    rank = warm_ref.shape[0]
    extra = rank * width // LANES
    pieces = sems.shape[0]
    per_piece = peers // pieces
    gets = []
    for piece in range(pieces):
        part = pl.ds(piece * per_piece * chunk, per_piece * chunk)
        gets.append(
            (
                pltpu.make_async_copy(gradient_ref.at[:, part], gradient_tile.at[:, part], sems.at[piece, 0]),
                pltpu.make_async_copy(error_ref.at[:, part], error_tile.at[:, part], sems.at[piece, 1]),
            )
        )
    warm_get = pltpu.make_async_copy(warm_ref, warm_tile, sems.at[0, 2])
    warm_get.start()
    for pair in gets:
        pair[0].start()
        pair[1].start()
    warm_get.wait()
    packed = jnp.concatenate(
        [warm_tile[i : i + extra] for i in range(0, rank, extra)], axis=1
    ).astype(BF16)
    for piece in range(pieces):
        gets[piece][0].wait()
        gets[piece][1].wait()
        for peer in range(piece * per_piece, (piece + 1) * per_piece):
            for i in range(chunk // LANES):
                part = slice(peer * chunk + i * LANES, peer * chunk + (i + 1) * LANES)
                tile = gradient_tile[:, part].astype(F32) + error_tile[:, part].astype(F32)
                send_ref[peer, i * width : (i + 1) * width, :] = tile.astype(BF16)
            send_ref[peer, tall - extra :, :] = packed


def rows_kernel(groups, width, scale, got_ref, mean_ref, send_ref):
    peers, tall, _ = got_ref.shape
    chunk = mean_ref.shape[1]
    high = width * chunk // LANES
    replicas = peers // groups
    warm = []
    for group in range(groups):
        total = got_ref[group, 0:high, :].astype(F32)
        for replica in range(1, replicas):
            total += got_ref[replica * groups + group, 0:high, :].astype(F32)
        total *= scale
        for i in range(chunk // LANES):
            mean_ref[group * width : (group + 1) * width, i * LANES : (i + 1) * LANES] = total[
                i * width : (i + 1) * width
            ]
        packed = got_ref[group, high:, :].astype(F32)
        warm.append(
            jnp.concatenate([packed[:, i : i + width] for i in range(0, LANES, width)], axis=0)
        )
    rows = jnp.dot(
        jnp.concatenate(warm, axis=1), mean_ref[...], precision=HIGHEST, preferred_element_type=F32
    ).astype(BF16)
    for peer in range(send_ref.shape[0]):
        send_ref[peer] = rows


def add(got_ref):
    total = got_ref[0].astype(F32)
    for peer in range(1, got_ref.shape[0]):
        total += got_ref[peer].astype(F32)
    return total.astype(BF16)


def columns_kernel(groups, got_ref, mean_ref, send_ref):
    rank, chunk = got_ref.shape[1:]
    half = rank // 2
    rows = add(got_ref)
    product = lax.dot_general(
        rows.astype(F32),
        mean_ref[...],
        (((1,), (1,)), ((), ())),
        precision=HIGHEST,
        preferred_element_type=F32,
    )
    width = product.shape[1] // groups
    for group in range(groups):
        high, low = split(product[:, group * width : (group + 1) * width], 2)
        tail = jnp.concatenate([high[:half], high[half:], low[:half], low[half:]], axis=1)
        for replica in range(send_ref.shape[0] // groups):
            peer = replica * groups + group
            for i in range(chunk // LANES):
                send_ref[peer, i * rank : (i + 1) * rank, :] = rows[:, i * LANES : (i + 1) * LANES]
            send_ref[peer, chunk // LANES * rank :, :] = tail


def eliminate(gram, product):
    rank, width = product.shape
    columns = [
        jnp.broadcast_to(gram[8 * (j // 8) :, j : j + 1], (rank - 8 * (j // 8), LANES))
        for j in range(rank)
    ]
    line = lax.broadcasted_iota(jnp.int32, (rank, LANES), 0)
    lane = lax.broadcasted_iota(jnp.int32, (rank, LANES), 1)
    work = jnp.concatenate([product, jnp.zeros((rank, LANES - width), F32)], axis=1)
    work = jnp.where(lane == line + width, 1.0, work)
    for k in range(rank):
        top = 8 * (k // 8)
        column = columns[k]
        inverse_root = lax.rsqrt(column[k - top : k - top + 1])
        column = column * inverse_root
        for j in range(k + 1, rank):
            first = 8 * (j // 8) - top
            columns[j] = columns[j] - column[first:] * column[j - top : j - top + 1]
        row = work[k : k + 1] * inverse_root
        rest = work[top:] - jnp.where(line[top:] > k, column, 0.0) * row
        rest = jnp.where(line[top:] == k, row, rest)
        work = jnp.concatenate([work[:top], rest], axis=0) if top else rest
    return work[:, width : width + rank], work[:, :width]


def factor_kernel(got_ref, next_ref, pair_ref, norm_ref):
    peers, tall, _ = got_ref.shape
    rank, width = next_ref.shape
    high = tall - rank // 2
    tails = [got_ref[peer, high:, :].astype(F32) for peer in range(peers)]
    while len(tails) > 1:
        tails = [sum(tails[i + 1 : i + 2], tails[i]) for i in range(0, len(tails), 2)]
    tails = tails[0][:, : 2 * width] + tails[0][:, 2 * width :]
    product = jnp.concatenate([tails[:, :width], tails[:, width:]], axis=0)
    gram = jnp.zeros((rank, rank), F32)
    for first in range(0, peers, 8):
        rows = jnp.concatenate(
            [
                got_ref[peer, i : i + rank, :]
                for peer in range(first, min(first + 8, peers))
                for i in range(0, high, rank)
            ],
            axis=1,
        )
        gram += lax.dot_general(rows, rows, (((1,), (1,)), ((), ())), preferred_element_type=F32)
    line = lax.broadcasted_iota(jnp.int32, (rank, rank), 0)
    eye = (line == lax.broadcasted_iota(jnp.int32, (rank, rank), 1)).astype(F32)
    trace = jnp.sum(gram * eye)
    inverse, next_factor = eliminate(gram + (0.0001 * trace / rank) * eye, product)
    next_ref[...] = next_factor
    norm_ref[...] = jnp.full(norm_ref.shape, jnp.sum(next_factor * next_factor), F32)
    pair_ref[...] = jnp.concatenate(
        [next_factor, inverse, jnp.zeros((rank, LANES - width - rank), F32)], axis=1
    )


def residual_kernel(got_ref, pair_ref, gradient_ref, error_ref, decompressed_ref, next_ref):
    peers, tall, _ = got_ref.shape
    rank = pair_ref.shape[0]
    high = tall - rank // 2
    chunk = high // rank * LANES
    width = next_ref.shape[0]
    mix = lax.dot_general(
        pair_ref[:, :width],
        pair_ref[:, width : width + rank],
        (((0,), (0,)), ((), ())),
        precision=HIGHEST,
        preferred_element_type=F32,
    )
    mix = jnp.concatenate(split(mix, 3), axis=1)
    for peer in range(peers):
        part = slice(peer * chunk, (peer + 1) * chunk)
        rows = jnp.concatenate(
            [got_ref[peer, i : i + rank, :] for i in range(0, high, rank)], axis=1
        )
        decompressed = jnp.dot(
            mix, jnp.concatenate([rows, rows, rows], axis=0), preferred_element_type=F32
        )
        decompressed_ref[:, part] = decompressed
        tile = (gradient_ref[:, part].astype(F32) + error_ref[:, part].astype(F32)).astype(BF16)
        next_ref[:, part] = (tile.astype(F32) - decompressed).astype(BF16)


def clip_kernel(norm_limit, norms_ref, decompressed_ref, applied_ref, tile, sems):
    norm_sq = jnp.sum(norms_ref[...][:, 0:1])
    clip_scale = jnp.minimum(1.0, norm_limit * lax.rsqrt(jnp.full((1, 1), norm_sq + 1e-06, F32)))
    pieces = sems.shape[0]
    step = applied_ref.shape[1] // pieces
    puts = []
    for piece in range(pieces):
        part = pl.ds(piece * step, step)
        tile[:, part] = (clip_scale * decompressed_ref[:, part]).astype(BF16)
        put = pltpu.make_async_copy(tile.at[:, part], applied_ref.at[:, part], sems.at[piece])
        put.start()
        puts.append(put)
    for put in puts:
        put.wait()


def call(kernel, outs, *args, vmem=16, spaces=None, out_space=pltpu.VMEM, scratch=(), cost=None):
    spaces = spaces or [pltpu.VMEM] * len(args)
    return pl.pallas_call(
        kernel,
        out_shape=outs,
        in_specs=[pl.BlockSpec(memory_space=space) for space in spaces],
        out_specs=jax.tree.map(lambda _: pl.BlockSpec(memory_space=out_space), outs),
        scratch_shapes=scratch,
        compiler_params=pltpu.CompilerParams(vmem_limit_bytes=vmem * 1024 * 1024),
        cost_estimate=cost,
    )(*args)


def per_device(gradient, error_buffer, warm_factor):
    shape = jax.ShapeDtypeStruct
    replicas, far, near, groups = (lax.axis_size(axis) for axis in ("gx", "far", "near", "gz"))
    plane, groups, columns = ("gx", "near", "gz"), near * groups, far * near * groups
    gradient, error_buffer = gradient[0], error_buffer[0]
    width, row_count = gradient.shape
    rank = warm_factor.shape[0]
    peers = replicas * groups
    chunk = row_count // peers
    norm_limit = 0.1 * math.sqrt(width * columns * row_count)
    pieces = min(4, peers)
    message = shape((peers, (width * chunk + rank * width) // LANES, LANES), BF16)

    send = call(
        merge_kernel,
        message,
        *(
            pltpu.with_memory_space_constraint(x, pltpu.HBM)
            for x in (gradient, error_buffer, warm_factor)
        ),
        spaces=[pltpu.HBM] * 3,
        scratch=[
            pltpu.VMEM((width, row_count), BF16),
            pltpu.VMEM((width, row_count), BF16),
            pltpu.VMEM((rank, width), F32),
            pltpu.SemaphoreType.DMA((pieces, 3)),
        ],
    )
    got = lax.all_to_all(send, plane, 0, 0)
    mean, send = call(
        lambda *refs: rows_kernel(groups, width, 1.0 / replicas, *refs),
        (shape((groups * width, chunk), F32), shape((far, rank, chunk), BF16)),
        got,
    )
    got = lax.all_to_all(send, "far", 0, 0)
    message = shape((peers, rank * chunk // LANES + rank // 2, LANES), BF16)
    send = call(lambda *refs: columns_kernel(groups, *refs), message, got, mean)
    got = lax.all_to_all(send, plane, 0, 0)
    next_factor, pair, norm = call(
        factor_kernel,
        (shape((rank, width), F32), shape((rank, LANES), F32), shape((columns, LANES), F32)),
        got,
    )
    norms = lax.all_to_all(norm, ("far", "near", "gz"), 0, 0, tiled=True)
    decompressed, next_error = call(
        residual_kernel,
        (shape((width, row_count), F32), shape((width, row_count), BF16)),
        got,
        pair,
        gradient,
        error_buffer,
        cost=pl.CostEstimate(
            flops=6 * rank * width * row_count, bytes_accessed=10 * width * row_count, transcendentals=0
        ),
    )
    applied = call(
        lambda *refs: clip_kernel(norm_limit, *refs),
        shape((width, row_count), BF16),
        norms,
        decompressed,
        out_space=pl.ANY,
        scratch=[pltpu.VMEM((width, row_count), BF16), pltpu.SemaphoreType.DMA((8,))],
    )
    return applied, next_error[None], next_factor


def solution(mesh):
    replicas, depth, groups = (mesh.shape[axis] for axis in ("gx", "gy", "gz"))
    near = math.gcd(depth, 2)
    fine = jax.sharding.Mesh(
        mesh.devices.reshape(replicas, depth // near, near, groups), ("gx", "far", "near", "gz")
    )
    columns = ("far", "near", "gz")
    in_specs = (P("gx", columns, None), P("gx", columns, None), P(None, columns))
    out_specs = (P(columns, None), P("gx", columns, None), P(None, columns))
    return jax.shard_map(
        per_device, mesh=fine, in_specs=in_specs, out_specs=out_specs, check_vma=False
    )
```

```python
import math

import jax
import jax.numpy as jnp
from jax import lax
from jax.experimental import pallas as pl
from jax.experimental.pallas import tpu as pltpu
from jax.sharding import PartitionSpec as P

F32 = jnp.float32
BF16 = jnp.bfloat16
HIGHEST = lax.Precision.HIGHEST
LANES = 128


def split(value, pieces):
    parts = []
    for _ in range(pieces):
        part = value.astype(BF16)
        parts.append(part)
        value = value - part.astype(F32)
    return parts


def merge_kernel(gradient_ref, error_ref, warm_ref, send_ref, gradient_tile, error_tile, warm_tile, sems):
    peers, tall, _ = send_ref.shape
    width, row_count = gradient_ref.shape
    chunk = row_count // peers
    rank = warm_ref.shape[0]
    extra = rank * width // LANES
    pieces = sems.shape[0]
    per_piece = peers // pieces
    gets = []
    for piece in range(pieces):
        part = pl.ds(piece * per_piece * chunk, per_piece * chunk)
        gets.append(
            (
                pltpu.make_async_copy(gradient_ref.at[:, part], gradient_tile.at[:, part], sems.at[piece, 0]),
                pltpu.make_async_copy(error_ref.at[:, part], error_tile.at[:, part], sems.at[piece, 1]),
            )
        )
    warm_get = pltpu.make_async_copy(warm_ref, warm_tile, sems.at[0, 2])
    warm_get.start()
    for pair in gets:
        pair[0].start()
        pair[1].start()
    warm_get.wait()
    packed = jnp.concatenate(
        [warm_tile[i : i + extra] for i in range(0, rank, extra)], axis=1
    ).astype(BF16)
    for piece in range(pieces):
        gets[piece][0].wait()
        gets[piece][1].wait()
        for peer in range(piece * per_piece, (piece + 1) * per_piece):
            for i in range(chunk // LANES):
                part = slice(peer * chunk + i * LANES, peer * chunk + (i + 1) * LANES)
                tile = gradient_tile[:, part].astype(F32) + error_tile[:, part].astype(F32)
                send_ref[peer, i * width : (i + 1) * width, :] = tile.astype(BF16)
            send_ref[peer, tall - extra :, :] = packed


def rows_kernel(groups, width, scale, got_ref, mean_ref, send_ref):
    peers, tall, _ = got_ref.shape
    chunk = mean_ref.shape[1]
    high = width * chunk // LANES
    replicas = peers // groups
    warm = []
    for group in range(groups):
        total = got_ref[group, 0:high, :].astype(F32)
        for replica in range(1, replicas):
            total += got_ref[replica * groups + group, 0:high, :].astype(F32)
        total *= scale
        for i in range(chunk // LANES):
            mean_ref[group * width : (group + 1) * width, i * LANES : (i + 1) * LANES] = total[
                i * width : (i + 1) * width
            ]
        packed = got_ref[group, high:, :].astype(F32)
        warm.append(
            jnp.concatenate([packed[:, i : i + width] for i in range(0, LANES, width)], axis=0)
        )
    rows = jnp.dot(
        jnp.concatenate(warm, axis=1), mean_ref[...], precision=HIGHEST, preferred_element_type=F32
    ).astype(BF16)
    for peer in range(send_ref.shape[0]):
        send_ref[peer] = rows


def add(got_ref):
    total = got_ref[0].astype(F32)
    for peer in range(1, got_ref.shape[0]):
        total += got_ref[peer].astype(F32)
    return total.astype(BF16)


def pack_gram(gram):
    half = gram.shape[0] // 2
    first, cross, second = gram[:half, :half], gram[:half, half:], gram[half:, half:]
    line = lax.broadcasted_iota(jnp.int32, (half, half), 0)
    lane = lax.broadcasted_iota(jnp.int32, (half, half), 1)
    diagonal = jnp.sum(jnp.where(line == lane, second, 0.0), axis=1, keepdims=True)
    return jnp.concatenate([jnp.where(line <= lane, first, second), diagonal, cross], axis=1)


def unpack_gram(packed):
    half = packed.shape[0]
    line = lax.broadcasted_iota(jnp.int32, (half, half), 0)
    lane = lax.broadcasted_iota(jnp.int32, (half, half), 1)
    both, diagonal, cross = packed[:, :half], packed[:, half : half + 1], packed[:, half + 1 :]
    first = jnp.where(line <= lane, both, 0.0)
    second = jnp.where(line > lane, both, jnp.where(line == lane, diagonal, 0.0))
    once = jnp.concatenate(
        [
            jnp.concatenate([first, cross], axis=1),
            jnp.concatenate([jnp.zeros((half, half), F32), second], axis=1),
        ],
        axis=0,
    )
    line = lax.broadcasted_iota(jnp.int32, (2 * half, 2 * half), 0)
    eye = line == lax.broadcasted_iota(jnp.int32, (2 * half, 2 * half), 1)
    turned = lax.dot_general(
        once,
        eye.astype(F32),
        (((0,), (0,)), ((), ())),
        precision=HIGHEST,
        preferred_element_type=F32,
    )
    return jnp.where(eye, once, once + turned)


def columns_kernel(groups, got_ref, mean_ref, send_ref):
    rank, chunk = got_ref.shape[1:]
    half = rank // 2
    replicas = send_ref.shape[0] // groups
    rows = add(got_ref)
    across = (((1,), (1,)), ((), ()))
    product = lax.dot_general(
        rows.astype(F32), mean_ref[...], across, precision=HIGHEST, preferred_element_type=F32
    )
    gram = lax.dot_general(rows, rows, across, preferred_element_type=F32)
    pieces = jnp.concatenate(split(pack_gram(gram), 3), axis=1)[:, : 3 * rank].astype(F32)
    rows = rows.astype(F32)
    share, block = rank // replicas, chunk // (half * replicas // rank)
    lower = []
    for replica in range(replicas):
        mine = rows[replica * share : (replica + 1) * share]
        mine = jnp.concatenate([mine[:, i : i + block] for i in range(0, chunk, block)], axis=0)
        lower.append(jnp.concatenate([pieces, mine], axis=1).astype(BF16))
    width = product.shape[1] // groups
    for group in range(groups):
        high, low = split(product[:, group * width : (group + 1) * width], 2)
        upper = jnp.concatenate([high[:half], high[half:], low[:half], low[half:]], axis=1)
        for replica in range(replicas):
            peer = replica * groups + group
            send_ref[peer, 0:half, :] = upper
            send_ref[peer, half:rank, :] = lower[replica]


def share_kernel(got_ref, share_ref):
    peers, rank, chunk = got_ref.shape
    share = share_ref.shape[0]
    half = rank // 2
    for peer in range(peers):
        mine = got_ref[peer, half:rank, 3 * rank :].astype(F32)
        mine = jnp.concatenate([mine[i : i + share] for i in range(0, half, share)], axis=1)
        share_ref[:, peer * chunk : (peer + 1) * chunk] = mine.astype(BF16)


def eliminate(gram, product):
    rank, width = product.shape
    columns = [
        jnp.broadcast_to(gram[8 * (j // 8) :, j : j + 1], (rank - 8 * (j // 8), LANES))
        for j in range(rank)
    ]
    line = lax.broadcasted_iota(jnp.int32, (rank, LANES), 0)
    lane = lax.broadcasted_iota(jnp.int32, (rank, LANES), 1)
    work = jnp.concatenate([product, jnp.zeros((rank, LANES - width), F32)], axis=1)
    work = jnp.where(lane == line + width, 1.0, work)
    for k in range(rank):
        top = 8 * (k // 8)
        column = columns[k]
        inverse_root = lax.rsqrt(column[k - top : k - top + 1])
        column = column * inverse_root
        for j in range(k + 1, rank):
            first = 8 * (j // 8) - top
            columns[j] = columns[j] - column[first:] * column[j - top : j - top + 1]
        row = work[k : k + 1] * inverse_root
        rest = work[top:] - jnp.where(line[top:] > k, column, 0.0) * row
        rest = jnp.where(line[top:] == k, row, rest)
        work = jnp.concatenate([work[:top], rest], axis=0) if top else rest
    return work[:, width : width + rank], work[:, :width]


def factor_kernel(got_ref, next_ref, pair_ref, norm_ref):
    rank, width = next_ref.shape
    half = rank // 2
    sums = [got_ref[peer].astype(F32) for peer in range(got_ref.shape[0])]
    while len(sums) > 1:
        sums = [sum(sums[i + 1 : i + 2], sums[i]) for i in range(0, len(sums), 2)]
    upper, lower = sums[0][:half], sums[0][half:]
    upper = upper[:, : 2 * width] + upper[:, 2 * width :]
    product = jnp.concatenate([upper[:, :width], upper[:, width:]], axis=0)
    third = jnp.concatenate(
        [lower[:, 2 * rank + 2 : 3 * rank], jnp.zeros((half, 3), F32)], axis=1
    )
    gram = unpack_gram(lower[:, : rank + 1] + lower[:, rank + 1 : 2 * rank + 2] + third)
    line = lax.broadcasted_iota(jnp.int32, (rank, rank), 0)
    eye = (line == lax.broadcasted_iota(jnp.int32, (rank, rank), 1)).astype(F32)
    trace = jnp.sum(gram * eye)
    inverse, next_factor = eliminate(gram + (0.0001 * trace / rank) * eye, product)
    next_ref[...] = next_factor
    norm_ref[...] = jnp.full(norm_ref.shape, jnp.sum(next_factor * next_factor), F32)
    pair_ref[...] = jnp.concatenate(
        [next_factor, inverse, jnp.zeros((rank, LANES - width - rank), F32)], axis=1
    )


def residual_kernel(shares_ref, pair_ref, gradient_ref, error_ref, decompressed_ref, next_ref):
    width, row_count = next_ref.shape
    rank = pair_ref.shape[0]
    mix = lax.dot_general(
        pair_ref[:, :width],
        pair_ref[:, width : width + rank],
        (((0,), (0,)), ((), ())),
        precision=HIGHEST,
        preferred_element_type=F32,
    )
    mix = jnp.concatenate(split(mix, 3), axis=1)
    step = 512
    for start in range(0, row_count, step):
        part = slice(start, start + step)
        rows = jnp.concatenate(
            [shares_ref[i, :, part].astype(F32) for i in range(shares_ref.shape[0])], axis=0
        ).astype(BF16)
        decompressed = jnp.dot(
            mix, jnp.concatenate([rows, rows, rows], axis=0), preferred_element_type=F32
        )
        decompressed_ref[:, part] = decompressed
        tile = (gradient_ref[:, part].astype(F32) + error_ref[:, part].astype(F32)).astype(BF16)
        next_ref[:, part] = (tile.astype(F32) - decompressed).astype(BF16)


def clip_kernel(norm_limit, norms_ref, decompressed_ref, applied_ref, tile, sems):
    norm_sq = jnp.sum(norms_ref[...][:, 0:1])
    clip_scale = jnp.minimum(1.0, norm_limit * lax.rsqrt(jnp.full((1, 1), norm_sq + 1e-06, F32)))
    pieces = sems.shape[0]
    step = applied_ref.shape[1] // pieces
    puts = []
    for piece in range(pieces):
        part = pl.ds(piece * step, step)
        tile[:, part] = (clip_scale * decompressed_ref[:, part]).astype(BF16)
        put = pltpu.make_async_copy(tile.at[:, part], applied_ref.at[:, part], sems.at[piece])
        put.start()
        puts.append(put)
    for put in puts:
        put.wait()


def call(kernel, outs, *args, vmem=16, spaces=None, out_space=pltpu.VMEM, scratch=(), cost=None):
    spaces = spaces or [pltpu.VMEM] * len(args)
    return pl.pallas_call(
        kernel,
        out_shape=outs,
        in_specs=[pl.BlockSpec(memory_space=space) for space in spaces],
        out_specs=jax.tree.map(lambda _: pl.BlockSpec(memory_space=out_space), outs),
        scratch_shapes=scratch,
        compiler_params=pltpu.CompilerParams(vmem_limit_bytes=vmem * 1024 * 1024),
        cost_estimate=cost,
    )(*args)


def per_device(gradient, error_buffer, warm_factor):
    shape = jax.ShapeDtypeStruct
    replicas, far, near, groups = (lax.axis_size(axis) for axis in ("gx", "far", "near", "gz"))
    plane, groups, columns = ("gx", "near", "gz"), near * groups, far * near * groups
    gradient, error_buffer = gradient[0], error_buffer[0]
    width, row_count = gradient.shape
    rank = warm_factor.shape[0]
    peers = replicas * groups
    chunk = row_count // peers
    norm_limit = 0.1 * math.sqrt(width * columns * row_count)
    pieces = min(4, peers)
    message = shape((peers, (width * chunk + rank * width) // LANES, LANES), BF16)

    send = call(
        merge_kernel,
        message,
        *(
            pltpu.with_memory_space_constraint(x, pltpu.HBM)
            for x in (gradient, error_buffer, warm_factor)
        ),
        spaces=[pltpu.HBM] * 3,
        scratch=[
            pltpu.VMEM((width, row_count), BF16),
            pltpu.VMEM((width, row_count), BF16),
            pltpu.VMEM((rank, width), F32),
            pltpu.SemaphoreType.DMA((pieces, 3)),
        ],
    )
    got = lax.all_to_all(send, plane, 0, 0)
    mean, send = call(
        lambda *refs: rows_kernel(groups, width, 1.0 / replicas, *refs),
        (shape((groups * width, chunk), F32), shape((far, rank, chunk), BF16)),
        got,
    )
    got = lax.all_to_all(send, "far", 0, 0)
    message = shape((peers, rank, LANES), BF16)
    send = call(lambda *refs: columns_kernel(groups, *refs), message, got, mean)
    got = lax.all_to_all(send, plane, 0, 0)
    next_factor, pair, norm = call(
        factor_kernel,
        (shape((rank, width), F32), shape((rank, LANES), F32), shape((columns, LANES), F32)),
        got,
    )
    norms = lax.all_to_all(norm, ("far", "near", "gz"), 0, 0, tiled=True)
    share = call(share_kernel, shape((rank // replicas, row_count), BF16), got)
    shares = lax.all_gather(share, "gx")
    decompressed, next_error = call(
        residual_kernel,
        (shape((width, row_count), F32), shape((width, row_count), BF16)),
        shares,
        pair,
        gradient,
        error_buffer,
        cost=pl.CostEstimate(
            flops=6 * rank * width * row_count, bytes_accessed=10 * width * row_count, transcendentals=0
        ),
    )
    applied = call(
        lambda *refs: clip_kernel(norm_limit, *refs),
        shape((width, row_count), BF16),
        norms,
        decompressed,
        out_space=pl.ANY,
        scratch=[pltpu.VMEM((width, row_count), BF16), pltpu.SemaphoreType.DMA((8,))],
    )
    return applied, next_error[None], next_factor


def solution(mesh):
    replicas, depth, groups = (mesh.shape[axis] for axis in ("gx", "gy", "gz"))
    near = math.gcd(depth, 2)
    fine = jax.sharding.Mesh(
        mesh.devices.reshape(replicas, depth // near, near, groups), ("gx", "far", "near", "gz")
    )
    columns = ("far", "near", "gz")
    in_specs = (P("gx", columns, None), P("gx", columns, None), P(None, columns))
    out_specs = (P(columns, None), P("gx", columns, None), P(None, columns))
    return jax.shard_map(
        per_device, mesh=fine, in_specs=in_specs, out_specs=out_specs, check_vma=False
    )
```

```python
import math

import jax
import jax.numpy as jnp
from jax import lax
from jax.experimental import pallas as pl
from jax.experimental.pallas import tpu as pltpu
from jax.sharding import PartitionSpec as P

F32 = jnp.float32
BF16 = jnp.bfloat16
HIGHEST = lax.Precision.HIGHEST
LANES = 128


def split(value, pieces):
    parts = []
    for _ in range(pieces):
        part = value.astype(BF16)
        parts.append(part)
        value = value - part.astype(F32)
    return parts


def merge_kernel(gradient_ref, error_ref, warm_ref, send_ref, gradient_tile, error_tile, warm_tile, sems):
    peers, tall, _ = send_ref.shape
    width, row_count = gradient_ref.shape
    chunk = row_count // peers
    rank = warm_ref.shape[0]
    extra = rank * width // LANES
    pieces = sems.shape[0]
    per_piece = peers // pieces
    gets = []
    for piece in range(pieces):
        part = pl.ds(piece * per_piece * chunk, per_piece * chunk)
        gets.append(
            (
                pltpu.make_async_copy(gradient_ref.at[:, part], gradient_tile.at[:, part], sems.at[piece, 0]),
                pltpu.make_async_copy(error_ref.at[:, part], error_tile.at[:, part], sems.at[piece, 1]),
            )
        )
    warm_get = pltpu.make_async_copy(warm_ref, warm_tile, sems.at[0, 2])
    warm_get.start()
    for pair in gets:
        pair[0].start()
        pair[1].start()
    warm_get.wait()
    packed = jnp.concatenate(
        [warm_tile[i : i + extra] for i in range(0, rank, extra)], axis=1
    ).astype(BF16)
    for piece in range(pieces):
        gets[piece][0].wait()
        gets[piece][1].wait()
        for peer in range(piece * per_piece, (piece + 1) * per_piece):
            for i in range(chunk // LANES):
                part = slice(peer * chunk + i * LANES, peer * chunk + (i + 1) * LANES)
                tile = gradient_tile[:, part].astype(F32) + error_tile[:, part].astype(F32)
                send_ref[peer, i * width : (i + 1) * width, :] = tile.astype(BF16)
            send_ref[peer, tall - extra :, :] = packed


def rows_kernel(groups, width, scale, got_ref, mean_ref, send_ref):
    peers, tall, _ = got_ref.shape
    chunk = mean_ref.shape[1]
    high = width * chunk // LANES
    replicas = peers // groups
    warm = []
    for group in range(groups):
        total = got_ref[group, 0:high, :].astype(F32)
        for replica in range(1, replicas):
            total += got_ref[replica * groups + group, 0:high, :].astype(F32)
        total *= scale
        for i in range(chunk // LANES):
            mean_ref[group * width : (group + 1) * width, i * LANES : (i + 1) * LANES] = total[
                i * width : (i + 1) * width
            ]
        packed = got_ref[group, high:, :].astype(F32)
        warm.append(
            jnp.concatenate([packed[:, i : i + width] for i in range(0, LANES, width)], axis=0)
        )
    rows = jnp.dot(
        jnp.concatenate(warm, axis=1), mean_ref[...], precision=HIGHEST, preferred_element_type=F32
    ).astype(BF16)
    for peer in range(send_ref.shape[0]):
        send_ref[peer] = rows


def add(got_ref):
    total = got_ref[0].astype(F32)
    for peer in range(1, got_ref.shape[0]):
        total += got_ref[peer].astype(F32)
    return total.astype(BF16)


def pack_gram(gram):
    half = gram.shape[0] // 2
    first, cross, second = gram[:half, :half], gram[:half, half:], gram[half:, half:]
    line = lax.broadcasted_iota(jnp.int32, (half, half), 0)
    lane = lax.broadcasted_iota(jnp.int32, (half, half), 1)
    diagonal = jnp.sum(jnp.where(line == lane, second, 0.0), axis=1, keepdims=True)
    return jnp.concatenate([jnp.where(line <= lane, first, second), diagonal, cross], axis=1)


def unpack_gram(packed):
    half = packed.shape[0]
    line = lax.broadcasted_iota(jnp.int32, (half, half), 0)
    lane = lax.broadcasted_iota(jnp.int32, (half, half), 1)
    both, diagonal, cross = packed[:, :half], packed[:, half : half + 1], packed[:, half + 1 :]
    first = jnp.where(line <= lane, both, 0.0)
    second = jnp.where(line > lane, both, jnp.where(line == lane, diagonal, 0.0))
    once = jnp.concatenate(
        [
            jnp.concatenate([first, cross], axis=1),
            jnp.concatenate([jnp.zeros((half, half), F32), second], axis=1),
        ],
        axis=0,
    )
    line = lax.broadcasted_iota(jnp.int32, (2 * half, 2 * half), 0)
    eye = line == lax.broadcasted_iota(jnp.int32, (2 * half, 2 * half), 1)
    turned = lax.dot_general(
        once,
        eye.astype(F32),
        (((0,), (0,)), ((), ())),
        precision=HIGHEST,
        preferred_element_type=F32,
    )
    return jnp.where(eye, once, once + turned)


def columns_kernel(groups, got_ref, mean_ref, send_ref):
    rank, chunk = got_ref.shape[1:]
    half = rank // 2
    replicas = send_ref.shape[0] // groups
    rows = add(got_ref)
    across = (((1,), (1,)), ((), ()))
    product = lax.dot_general(
        rows.astype(F32), mean_ref[...], across, precision=HIGHEST, preferred_element_type=F32
    )
    gram = lax.dot_general(rows, rows, across, preferred_element_type=F32)
    pieces = jnp.concatenate(split(pack_gram(gram), 3), axis=1)[:, : 3 * rank].astype(F32)
    rows = rows.astype(F32)
    share, block = rank // replicas, chunk // (half * replicas // rank)
    lower = []
    for replica in range(replicas):
        mine = rows[replica * share : (replica + 1) * share]
        mine = jnp.concatenate([mine[:, i : i + block] for i in range(0, chunk, block)], axis=0)
        lower.append(jnp.concatenate([pieces, mine], axis=1).astype(BF16))
    width = product.shape[1] // groups
    for group in range(groups):
        high, low = split(product[:, group * width : (group + 1) * width], 2)
        upper = jnp.concatenate([high[:half], high[half:], low[:half], low[half:]], axis=1)
        for replica in range(replicas):
            peer = replica * groups + group
            send_ref[peer, 0:half, :] = upper
            send_ref[peer, half:rank, :] = lower[replica]


def share_kernel(got_ref, share_ref):
    peers, rank, chunk = got_ref.shape
    share = share_ref.shape[0]
    half = rank // 2
    for peer in range(peers):
        mine = got_ref[peer, half:rank, 3 * rank :].astype(F32)
        mine = jnp.concatenate([mine[i : i + share] for i in range(0, half, share)], axis=1)
        share_ref[:, peer * chunk : (peer + 1) * chunk] = mine.astype(BF16)


def eliminate(gram, product):
    rank, width = product.shape
    columns = [
        jnp.broadcast_to(gram[8 * (j // 8) :, j : j + 1], (rank - 8 * (j // 8), LANES))
        for j in range(rank)
    ]
    line = lax.broadcasted_iota(jnp.int32, (rank, LANES), 0)
    lane = lax.broadcasted_iota(jnp.int32, (rank, LANES), 1)
    work = jnp.concatenate([product, jnp.zeros((rank, LANES - width), F32)], axis=1)
    work = jnp.where(lane == line + width, 1.0, work)
    for k in range(rank):
        top = 8 * (k // 8)
        column = columns[k]
        inverse_root = lax.rsqrt(column[k - top : k - top + 1])
        column = column * inverse_root
        for j in range(k + 1, rank):
            first = 8 * (j // 8) - top
            columns[j] = columns[j] - column[first:] * column[j - top : j - top + 1]
        row = work[k : k + 1] * inverse_root
        rest = work[top:] - jnp.where(line[top:] > k, column, 0.0) * row
        rest = jnp.where(line[top:] == k, row, rest)
        work = jnp.concatenate([work[:top], rest], axis=0) if top else rest
    return work[:, width : width + rank], work[:, :width]


def factor_kernel(got_ref, next_ref, pair_ref, norm_ref):
    rank, width = next_ref.shape
    half = rank // 2
    sums = [got_ref[peer].astype(F32) for peer in range(got_ref.shape[0])]
    while len(sums) > 1:
        sums = [sum(sums[i + 1 : i + 2], sums[i]) for i in range(0, len(sums), 2)]
    upper, lower = sums[0][:half], sums[0][half:]
    upper = upper[:, : 2 * width] + upper[:, 2 * width :]
    product = jnp.concatenate([upper[:, :width], upper[:, width:]], axis=0)
    third = jnp.concatenate(
        [lower[:, 2 * rank + 2 : 3 * rank], jnp.zeros((half, 3), F32)], axis=1
    )
    gram = unpack_gram(lower[:, : rank + 1] + lower[:, rank + 1 : 2 * rank + 2] + third)
    line = lax.broadcasted_iota(jnp.int32, (rank, rank), 0)
    eye = (line == lax.broadcasted_iota(jnp.int32, (rank, rank), 1)).astype(F32)
    trace = jnp.sum(gram * eye)
    inverse, next_factor = eliminate(gram + (0.0001 * trace / rank) * eye, product)
    next_ref[...] = next_factor
    norm_ref[...] = jnp.full(norm_ref.shape, jnp.sum(next_factor * next_factor), F32)
    pair_ref[...] = jnp.concatenate(
        [next_factor, inverse, jnp.zeros((rank, LANES - width - rank), F32)], axis=1
    )


def update_kernel(
    norm_limit, norms_ref, shares_ref, pair_ref, gradient_ref, error_ref, applied_ref, next_ref, applied_tile, next_tile, sems
):
    width, row_count = next_ref.shape
    rank = pair_ref.shape[0]
    mix = lax.dot_general(
        pair_ref[:, :width],
        pair_ref[:, width : width + rank],
        (((0,), (0,)), ((), ())),
        precision=HIGHEST,
        preferred_element_type=F32,
    )
    mix = jnp.concatenate(split(mix, 3), axis=1)
    norm_sq = jnp.sum(norms_ref[...][:, 0:1], axis=0, keepdims=True)
    clip_scale = jnp.minimum(1.0, norm_limit * lax.rsqrt(norm_sq + 1e-06))
    pieces = sems.shape[0]
    span = row_count // pieces
    step = min(512, span)
    puts = []
    for piece in range(pieces):
        for start in range(piece * span, (piece + 1) * span, step):
            part = slice(start, start + step)
            rows = jnp.concatenate(
                [shares_ref[i, :, part].astype(F32) for i in range(shares_ref.shape[0])], axis=0
            ).astype(BF16)
            decompressed = jnp.dot(
                mix, jnp.concatenate([rows, rows, rows], axis=0), preferred_element_type=F32
            )
            applied_tile[:, part] = (clip_scale * decompressed).astype(BF16)
            tile = (gradient_ref[:, part].astype(F32) + error_ref[:, part].astype(F32)).astype(BF16)
            next_tile[:, part] = (tile.astype(F32) - decompressed).astype(BF16)
        part = pl.ds(piece * span, span)
        for i, (source, target) in enumerate(((applied_tile, applied_ref), (next_tile, next_ref))):
            put = pltpu.make_async_copy(source.at[:, part], target.at[:, part], sems.at[piece, i])
            put.start()
            puts.append(put)
    for put in puts:
        put.wait()


def call(kernel, outs, *args, vmem=16, spaces=None, out_space=pltpu.VMEM, scratch=(), cost=None):
    spaces = spaces or [pltpu.VMEM] * len(args)
    return pl.pallas_call(
        kernel,
        out_shape=outs,
        in_specs=[pl.BlockSpec(memory_space=space) for space in spaces],
        out_specs=jax.tree.map(lambda _: pl.BlockSpec(memory_space=out_space), outs),
        scratch_shapes=scratch,
        compiler_params=pltpu.CompilerParams(vmem_limit_bytes=vmem * 1024 * 1024),
        cost_estimate=cost,
    )(*args)


def per_device(gradient, error_buffer, warm_factor):
    shape = jax.ShapeDtypeStruct
    replicas, far, near, groups = (lax.axis_size(axis) for axis in ("gx", "far", "near", "gz"))
    plane, groups, columns = ("gx", "near", "gz"), near * groups, far * near * groups
    gradient, error_buffer = gradient[0], error_buffer[0]
    width, row_count = gradient.shape
    rank = warm_factor.shape[0]
    peers = replicas * groups
    chunk = row_count // peers
    norm_limit = 0.1 * math.sqrt(width * columns * row_count)
    pieces = min(4, peers)
    message = shape((peers, (width * chunk + rank * width) // LANES, LANES), BF16)

    send = call(
        merge_kernel,
        message,
        *(
            pltpu.with_memory_space_constraint(x, pltpu.HBM)
            for x in (gradient, error_buffer, warm_factor)
        ),
        spaces=[pltpu.HBM] * 3,
        scratch=[
            pltpu.VMEM((width, row_count), BF16),
            pltpu.VMEM((width, row_count), BF16),
            pltpu.VMEM((rank, width), F32),
            pltpu.SemaphoreType.DMA((pieces, 3)),
        ],
    )
    got = lax.all_to_all(send, plane, 0, 0)
    mean, send = call(
        lambda *refs: rows_kernel(groups, width, 1.0 / replicas, *refs),
        (shape((groups * width, chunk), F32), shape((far, rank, chunk), BF16)),
        got,
    )
    got = lax.all_to_all(send, "far", 0, 0)
    message = shape((peers, rank, LANES), BF16)
    send = call(lambda *refs: columns_kernel(groups, *refs), message, got, mean)
    got = lax.all_to_all(send, plane, 0, 0)
    next_factor, pair, norm = call(
        factor_kernel,
        (shape((rank, width), F32), shape((rank, LANES), F32), shape((columns, LANES), F32)),
        got,
    )
    norms = lax.all_to_all(norm, ("far", "near", "gz"), 0, 0, tiled=True)
    share = call(share_kernel, shape((rank // replicas, row_count), BF16), got)
    shares = lax.all_gather(share, "gx")
    applied, next_error = call(
        lambda *refs: update_kernel(norm_limit, *refs),
        (shape((width, row_count), BF16), shape((width, row_count), BF16)),
        norms,
        shares,
        pair,
        gradient,
        error_buffer,
        out_space=pl.ANY,
        scratch=[
            pltpu.VMEM((width, row_count), BF16),
            pltpu.VMEM((width, row_count), BF16),
            pltpu.SemaphoreType.DMA((4, 2)),
        ],
    )
    return applied, next_error[None], next_factor


def solution(mesh):
    replicas, depth, groups = (mesh.shape[axis] for axis in ("gx", "gy", "gz"))
    near = math.gcd(depth, 2)
    fine = jax.sharding.Mesh(
        mesh.devices.reshape(replicas, depth // near, near, groups), ("gx", "far", "near", "gz")
    )
    columns = ("far", "near", "gz")
    in_specs = (P("gx", columns, None), P("gx", columns, None), P(None, columns))
    out_specs = (P(columns, None), P("gx", columns, None), P(None, columns))
    return jax.shard_map(
        per_device, mesh=fine, in_specs=in_specs, out_specs=out_specs, check_vma=False
    )
```

```python
import math

import jax
import jax.numpy as jnp
from jax import lax
from jax.experimental import pallas as pl
from jax.experimental.pallas import tpu as pltpu
from jax.sharding import PartitionSpec as P

F32 = jnp.float32
BF16 = jnp.bfloat16
HIGHEST = lax.Precision.HIGHEST
LANES = 128


def split(value, pieces):
    parts = []
    for _ in range(pieces):
        part = value.astype(BF16)
        parts.append(part)
        value = value - part.astype(F32)
    return parts


def merge_kernel(gradient_ref, error_ref, warm_ref, send_ref, gradient_tile, error_tile, warm_tile, sems):
    peers, tall, _ = send_ref.shape
    width, row_count = gradient_ref.shape
    chunk = row_count // peers
    rank = warm_ref.shape[0]
    extra = rank * width // LANES
    pieces = sems.shape[0]
    per_piece = peers // pieces
    gets = []
    for piece in range(pieces):
        part = pl.ds(piece * per_piece * chunk, per_piece * chunk)
        gets.append(
            (
                pltpu.make_async_copy(gradient_ref.at[:, part], gradient_tile.at[:, part], sems.at[piece, 0]),
                pltpu.make_async_copy(error_ref.at[:, part], error_tile.at[:, part], sems.at[piece, 1]),
            )
        )
    warm_get = pltpu.make_async_copy(warm_ref, warm_tile, sems.at[0, 2])
    warm_get.start()
    for pair in gets:
        pair[0].start()
        pair[1].start()
    warm_get.wait()
    packed = jnp.concatenate(
        [warm_tile[i : i + extra] for i in range(0, rank, extra)], axis=1
    ).astype(BF16)
    for piece in range(pieces):
        gets[piece][0].wait()
        gets[piece][1].wait()
        for peer in range(piece * per_piece, (piece + 1) * per_piece):
            for i in range(chunk // LANES):
                part = slice(peer * chunk + i * LANES, peer * chunk + (i + 1) * LANES)
                tile = gradient_tile[:, part].astype(F32) + error_tile[:, part].astype(F32)
                send_ref[peer, i * width : (i + 1) * width, :] = tile.astype(BF16)
            send_ref[peer, tall - extra :, :] = packed


def rows_kernel(groups, width, scale, got_ref, mean_ref, send_ref):
    peers, tall, _ = got_ref.shape
    chunk = mean_ref.shape[1]
    high = width * chunk // LANES
    replicas = peers // groups
    warm = []
    for group in range(groups):
        total = got_ref[group, 0:high, :].astype(F32)
        for replica in range(1, replicas):
            total += got_ref[replica * groups + group, 0:high, :].astype(F32)
        total *= scale
        for i in range(chunk // LANES):
            mean_ref[group * width : (group + 1) * width, i * LANES : (i + 1) * LANES] = total[
                i * width : (i + 1) * width
            ]
        packed = got_ref[group, high:, :].astype(F32)
        warm.append(
            jnp.concatenate([packed[:, i : i + width] for i in range(0, LANES, width)], axis=0)
        )
    rows = jnp.dot(
        jnp.concatenate(warm, axis=1), mean_ref[...], precision=HIGHEST, preferred_element_type=F32
    ).astype(BF16)
    for peer in range(send_ref.shape[0]):
        send_ref[peer] = rows


def add(got_ref):
    total = got_ref[0].astype(F32)
    for peer in range(1, got_ref.shape[0]):
        total += got_ref[peer].astype(F32)
    return total.astype(BF16)


def pack_gram(gram):
    half = gram.shape[0] // 2
    first, cross, second = gram[:half, :half], gram[:half, half:], gram[half:, half:]
    line = lax.broadcasted_iota(jnp.int32, (half, half), 0)
    lane = lax.broadcasted_iota(jnp.int32, (half, half), 1)
    diagonal = jnp.sum(jnp.where(line == lane, second, 0.0), axis=1, keepdims=True)
    return jnp.concatenate([jnp.where(line <= lane, first, second), diagonal, cross], axis=1)


def unpack_gram(packed):
    half = packed.shape[0]
    line = lax.broadcasted_iota(jnp.int32, (half, half), 0)
    lane = lax.broadcasted_iota(jnp.int32, (half, half), 1)
    both, diagonal, cross = packed[:, :half], packed[:, half : half + 1], packed[:, half + 1 :]
    first = jnp.where(line <= lane, both, 0.0)
    second = jnp.where(line > lane, both, jnp.where(line == lane, diagonal, 0.0))
    once = jnp.concatenate(
        [
            jnp.concatenate([first, cross], axis=1),
            jnp.concatenate([jnp.zeros((half, half), F32), second], axis=1),
        ],
        axis=0,
    )
    line = lax.broadcasted_iota(jnp.int32, (2 * half, 2 * half), 0)
    eye = line == lax.broadcasted_iota(jnp.int32, (2 * half, 2 * half), 1)
    return jnp.where(eye, once, once + once.T)


def columns_kernel(groups, got_ref, mean_ref, send_ref):
    rank, chunk = got_ref.shape[1:]
    half = rank // 2
    replicas = send_ref.shape[0] // groups
    rows = add(got_ref)
    across = (((1,), (1,)), ((), ()))
    product = lax.dot_general(
        rows.astype(F32), mean_ref[...], across, precision=HIGHEST, preferred_element_type=F32
    )
    gram = lax.dot_general(rows, rows, across, preferred_element_type=F32)
    pieces = jnp.concatenate(split(pack_gram(gram), 3), axis=1)[:, : 3 * rank].astype(F32)
    rows = rows.astype(F32)
    share, block = rank // replicas, chunk // (half * replicas // rank)
    lower = []
    for replica in range(replicas):
        mine = rows[replica * share : (replica + 1) * share]
        mine = jnp.concatenate([mine[:, i : i + block] for i in range(0, chunk, block)], axis=0)
        lower.append(jnp.concatenate([pieces, mine], axis=1).astype(BF16))
    width = product.shape[1] // groups
    for group in range(groups):
        high, low = split(product[:, group * width : (group + 1) * width], 2)
        upper = jnp.concatenate([high[:half], high[half:], low[:half], low[half:]], axis=1)
        for replica in range(replicas):
            peer = replica * groups + group
            send_ref[peer, 0:half, :] = upper
            send_ref[peer, half:rank, :] = lower[replica]


def eliminate(gram, product):
    rank, width = product.shape
    columns = [
        jnp.broadcast_to(gram[8 * (j // 8) :, j : j + 1], (rank - 8 * (j // 8), LANES))
        for j in range(rank)
    ]
    line = lax.broadcasted_iota(jnp.int32, (rank, LANES), 0)
    lane = lax.broadcasted_iota(jnp.int32, (rank, LANES), 1)
    work = jnp.concatenate([product, jnp.zeros((rank, LANES - width), F32)], axis=1)
    work = jnp.where(lane == line + width, 1.0, work)
    for k in range(rank):
        top = 8 * (k // 8)
        column = columns[k]
        inverse_root = lax.rsqrt(column[k - top : k - top + 1])
        column = column * inverse_root
        for j in range(k + 1, rank):
            first = 8 * (j // 8) - top
            columns[j] = columns[j] - column[first:] * column[j - top : j - top + 1]
        row = work[k : k + 1] * inverse_root
        rest = work[top:] - jnp.where(line[top:] > k, column, 0.0) * row
        rest = jnp.where(line[top:] == k, row, rest)
        work = jnp.concatenate([work[:top], rest], axis=0) if top else rest
    return work[:, width : width + rank], work[:, :width]


def factor_kernel(got_ref, next_ref, pair_ref, norm_ref, share_ref):
    rank, width = next_ref.shape
    half = rank // 2
    peers, _, chunk = got_ref.shape
    share = share_ref.shape[0]
    for peer in range(peers):
        mine = got_ref[peer, half:rank, 3 * rank :].astype(F32)
        mine = jnp.concatenate([mine[i : i + share] for i in range(0, half, share)], axis=1)
        share_ref[:, peer * chunk : (peer + 1) * chunk] = mine.astype(BF16)
    sums = [got_ref[peer].astype(F32) for peer in range(peers)]
    while len(sums) > 1:
        sums = [sum(sums[i + 1 : i + 2], sums[i]) for i in range(0, len(sums), 2)]
    upper, lower = sums[0][:half], sums[0][half:]
    upper = upper[:, : 2 * width] + upper[:, 2 * width :]
    product = jnp.concatenate([upper[:, :width], upper[:, width:]], axis=0)
    third = jnp.concatenate(
        [lower[:, 2 * rank + 2 : 3 * rank], jnp.zeros((half, 3), F32)], axis=1
    )
    gram = unpack_gram(lower[:, : rank + 1] + lower[:, rank + 1 : 2 * rank + 2] + third)
    line = lax.broadcasted_iota(jnp.int32, (rank, rank), 0)
    eye = (line == lax.broadcasted_iota(jnp.int32, (rank, rank), 1)).astype(F32)
    trace = jnp.sum(gram * eye)
    inverse, next_factor = eliminate(gram + (0.0001 * trace / rank) * eye, product)
    next_ref[...] = next_factor
    norm_ref[...] = jnp.full(norm_ref.shape, jnp.sum(next_factor * next_factor), F32)
    pair_ref[...] = jnp.concatenate(
        [next_factor, inverse, jnp.zeros((rank, LANES - width - rank), F32)], axis=1
    )


def update_kernel(
    norm_limit, norms_ref, shares_ref, pair_ref, gradient_ref, error_ref, applied_ref, next_ref, applied_tile, next_tile, sems
):
    width, row_count = next_ref.shape
    rank = pair_ref.shape[0]
    mix = lax.dot_general(
        pair_ref[:, :width],
        pair_ref[:, width : width + rank],
        (((0,), (0,)), ((), ())),
        precision=HIGHEST,
        preferred_element_type=F32,
    )
    mix = jnp.concatenate(split(mix, 3), axis=1)
    norm_sq = jnp.sum(norms_ref[...][:, 0:1], axis=0, keepdims=True)
    clip_scale = jnp.minimum(1.0, norm_limit * lax.rsqrt(norm_sq + 1e-06))
    pieces = sems.shape[0]
    span = row_count // pieces
    step = min(512, span)
    puts = []
    for piece in range(pieces):
        for start in range(piece * span, (piece + 1) * span, step):
            part = slice(start, start + step)
            rows = jnp.concatenate(
                [shares_ref[i, :, part].astype(F32) for i in range(shares_ref.shape[0])], axis=0
            ).astype(BF16)
            decompressed = jnp.dot(
                mix, jnp.concatenate([rows, rows, rows], axis=0), preferred_element_type=F32
            )
            applied_tile[:, part] = (clip_scale * decompressed).astype(BF16)
            tile = (gradient_ref[:, part].astype(F32) + error_ref[:, part].astype(F32)).astype(BF16)
            next_tile[:, part] = (tile.astype(F32) - decompressed).astype(BF16)
        part = pl.ds(piece * span, span)
        for i, (source, target) in enumerate(((applied_tile, applied_ref), (next_tile, next_ref))):
            put = pltpu.make_async_copy(source.at[:, part], target.at[:, part], sems.at[piece, i])
            put.start()
            puts.append(put)
    for put in puts:
        put.wait()


def call(kernel, outs, *args, vmem=16, spaces=None, out_space=pltpu.VMEM, scratch=(), cost=None):
    spaces = spaces or [pltpu.VMEM] * len(args)
    return pl.pallas_call(
        kernel,
        out_shape=outs,
        in_specs=[pl.BlockSpec(memory_space=space) for space in spaces],
        out_specs=jax.tree.map(lambda _: pl.BlockSpec(memory_space=out_space), outs),
        scratch_shapes=scratch,
        compiler_params=pltpu.CompilerParams(vmem_limit_bytes=vmem * 1024 * 1024),
        cost_estimate=cost,
    )(*args)


def per_device(gradient, error_buffer, warm_factor):
    shape = jax.ShapeDtypeStruct
    replicas, far, near, groups = (lax.axis_size(axis) for axis in ("gx", "far", "near", "gz"))
    plane, groups, columns = ("gx", "near", "gz"), near * groups, far * near * groups
    gradient, error_buffer = gradient[0], error_buffer[0]
    width, row_count = gradient.shape
    rank = warm_factor.shape[0]
    peers = replicas * groups
    chunk = row_count // peers
    norm_limit = 0.1 * math.sqrt(width * columns * row_count)
    pieces = min(4, peers)
    message = shape((peers, (width * chunk + rank * width) // LANES, LANES), BF16)

    send = call(
        merge_kernel,
        message,
        *(
            pltpu.with_memory_space_constraint(x, pltpu.HBM)
            for x in (gradient, error_buffer, warm_factor)
        ),
        spaces=[pltpu.HBM] * 3,
        scratch=[
            pltpu.VMEM((width, row_count), BF16),
            pltpu.VMEM((width, row_count), BF16),
            pltpu.VMEM((rank, width), F32),
            pltpu.SemaphoreType.DMA((pieces, 3)),
        ],
    )
    got = lax.all_to_all(send, plane, 0, 0)
    mean, send = call(
        lambda *refs: rows_kernel(groups, width, 1.0 / replicas, *refs),
        (shape((groups * width, chunk), F32), shape((far, rank, chunk), BF16)),
        got,
    )
    got = lax.all_to_all(send, "far", 0, 0)
    message = shape((peers, rank, LANES), BF16)
    send = call(lambda *refs: columns_kernel(groups, *refs), message, got, mean)
    got = lax.all_to_all(send, plane, 0, 0)
    next_factor, pair, norm, share = call(
        factor_kernel,
        (
            shape((rank, width), F32),
            shape((rank, LANES), F32),
            shape((columns, LANES), F32),
            shape((rank // replicas, row_count), BF16),
        ),
        got,
    )
    norms = lax.all_to_all(norm, ("far", "near", "gz"), 0, 0, tiled=True)
    shares = lax.all_gather(share, "gx")
    applied, next_error = call(
        lambda *refs: update_kernel(norm_limit, *refs),
        (shape((width, row_count), BF16), shape((width, row_count), BF16)),
        norms,
        shares,
        pair,
        gradient,
        error_buffer,
        out_space=pl.ANY,
        scratch=[
            pltpu.VMEM((width, row_count), BF16),
            pltpu.VMEM((width, row_count), BF16),
            pltpu.SemaphoreType.DMA((4, 2)),
        ],
    )
    return applied, next_error[None], next_factor


def solution(mesh):
    replicas, depth, groups = (mesh.shape[axis] for axis in ("gx", "gy", "gz"))
    near = math.gcd(depth, 2)
    fine = jax.sharding.Mesh(
        mesh.devices.reshape(replicas, depth // near, near, groups), ("gx", "far", "near", "gz")
    )
    columns = ("far", "near", "gz")
    in_specs = (P("gx", columns, None), P("gx", columns, None), P(None, columns))
    out_specs = (P(columns, None), P("gx", columns, None), P(None, columns))
    return jax.shard_map(
        per_device, mesh=fine, in_specs=in_specs, out_specs=out_specs, check_vma=False
    )
```

```python
import math

import jax
import jax.numpy as jnp
from jax import lax
from jax.experimental import pallas as pl
from jax.experimental.pallas import tpu as pltpu
from jax.sharding import PartitionSpec as P

F32 = jnp.float32
BF16 = jnp.bfloat16
HIGHEST = lax.Precision.HIGHEST
LANES = 128


def split(value, pieces):
    parts = []
    for _ in range(pieces):
        part = value.astype(BF16)
        parts.append(part)
        value = value - part.astype(F32)
    return parts


def merge_kernel(gradient_ref, error_ref, warm_ref, send_ref, gradient_tile, error_tile, warm_tile, sems):
    peers, tall, _ = send_ref.shape
    width, row_count = gradient_ref.shape
    chunk = row_count // peers
    rank = warm_ref.shape[0]
    extra = rank * width // LANES
    pieces = sems.shape[0]
    per_piece = peers // pieces
    gets = []
    for piece in range(pieces):
        part = pl.ds(piece * per_piece * chunk, per_piece * chunk)
        gets.append(
            (
                pltpu.make_async_copy(gradient_ref.at[:, part], gradient_tile.at[:, part], sems.at[piece, 0]),
                pltpu.make_async_copy(error_ref.at[:, part], error_tile.at[:, part], sems.at[piece, 1]),
            )
        )
    warm_get = pltpu.make_async_copy(warm_ref, warm_tile, sems.at[0, 2])
    warm_get.start()
    for pair in gets:
        pair[0].start()
        pair[1].start()
    warm_get.wait()
    packed = jnp.concatenate(
        [warm_tile[i : i + extra] for i in range(0, rank, extra)], axis=1
    ).astype(BF16)
    for piece in range(pieces):
        gets[piece][0].wait()
        gets[piece][1].wait()
        for peer in range(piece * per_piece, (piece + 1) * per_piece):
            for i in range(chunk // LANES):
                part = slice(peer * chunk + i * LANES, peer * chunk + (i + 1) * LANES)
                tile = gradient_tile[:, part].astype(F32) + error_tile[:, part].astype(F32)
                send_ref[peer, i * width : (i + 1) * width, :] = tile.astype(BF16)
            send_ref[peer, tall - extra :, :] = packed


def rows_kernel(groups, width, scale, got_ref, mean_ref, send_ref):
    peers, tall, _ = got_ref.shape
    chunk = mean_ref.shape[1]
    high = width * chunk // LANES
    replicas = peers // groups
    warm = []
    for group in range(groups):
        total = got_ref[group, 0:high, :].astype(F32)
        for replica in range(1, replicas):
            total += got_ref[replica * groups + group, 0:high, :].astype(F32)
        total *= scale
        for i in range(chunk // LANES):
            mean_ref[group * width : (group + 1) * width, i * LANES : (i + 1) * LANES] = total[
                i * width : (i + 1) * width
            ]
        packed = got_ref[group, high:, :].astype(F32)
        warm.append(
            jnp.concatenate([packed[:, i : i + width] for i in range(0, LANES, width)], axis=0)
        )
    rows = jnp.dot(
        jnp.concatenate(warm, axis=1), mean_ref[...], precision=HIGHEST, preferred_element_type=F32
    ).astype(BF16)
    for peer in range(send_ref.shape[0]):
        send_ref[peer] = rows


def add(got_ref):
    total = got_ref[0].astype(F32)
    for peer in range(1, got_ref.shape[0]):
        total += got_ref[peer].astype(F32)
    return total.astype(BF16)


def pack_gram(gram):
    half = gram.shape[0] // 2
    first, cross, second = gram[:half, :half], gram[:half, half:], gram[half:, half:]
    line = lax.broadcasted_iota(jnp.int32, (half, half), 0)
    lane = lax.broadcasted_iota(jnp.int32, (half, half), 1)
    diagonal = jnp.sum(jnp.where(line == lane, second, 0.0), axis=1, keepdims=True)
    return jnp.concatenate([jnp.where(line <= lane, first, second), diagonal, cross], axis=1)


def unpack_gram(packed):
    half = packed.shape[0]
    line = lax.broadcasted_iota(jnp.int32, (half, half), 0)
    lane = lax.broadcasted_iota(jnp.int32, (half, half), 1)
    both, diagonal, cross = packed[:, :half], packed[:, half : half + 1], packed[:, half + 1 :]
    first = jnp.where(line <= lane, both, 0.0)
    second = jnp.where(line > lane, both, jnp.where(line == lane, diagonal, 0.0))
    once = jnp.concatenate(
        [
            jnp.concatenate([first, cross], axis=1),
            jnp.concatenate([jnp.zeros((half, half), F32), second], axis=1),
        ],
        axis=0,
    )
    line = lax.broadcasted_iota(jnp.int32, (2 * half, 2 * half), 0)
    eye = line == lax.broadcasted_iota(jnp.int32, (2 * half, 2 * half), 1)
    return jnp.where(eye, once, once + once.T)


def columns_kernel(groups, got_ref, mean_ref, send_ref):
    rank, chunk = got_ref.shape[1:]
    half = rank // 2
    replicas = send_ref.shape[0] // groups
    rows = add(got_ref)
    across = (((1,), (1,)), ((), ()))
    product = lax.dot_general(
        rows.astype(F32), mean_ref[...], across, precision=HIGHEST, preferred_element_type=F32
    )
    gram = lax.dot_general(rows, rows, across, preferred_element_type=F32)
    pieces = jnp.concatenate(split(pack_gram(gram), 3), axis=1)[:, : 3 * rank].astype(F32)
    rows = rows.astype(F32)
    share, block = rank // replicas, chunk // (half * replicas // rank)
    lower = []
    for replica in range(replicas):
        mine = rows[replica * share : (replica + 1) * share]
        mine = jnp.concatenate([mine[:, i : i + block] for i in range(0, chunk, block)], axis=0)
        lower.append(jnp.concatenate([pieces, mine], axis=1).astype(BF16))
    width = product.shape[1] // groups
    for group in range(groups):
        high, low = split(product[:, group * width : (group + 1) * width], 2)
        upper = jnp.concatenate([high[:half], high[half:], low[:half], low[half:]], axis=1)
        for replica in range(replicas):
            peer = replica * groups + group
            send_ref[peer, 0:half, :] = upper
            send_ref[peer, half:rank, :] = lower[replica]


def eliminate(gram, product):
    rank, width = product.shape
    columns = [
        jnp.broadcast_to(gram[8 * (j // 8) :, j : j + 1], (rank - 8 * (j // 8), LANES))
        for j in range(rank)
    ]
    line = lax.broadcasted_iota(jnp.int32, (rank, LANES), 0)
    lane = lax.broadcasted_iota(jnp.int32, (rank, LANES), 1)
    work = jnp.concatenate([product, jnp.zeros((rank, LANES - width), F32)], axis=1)
    work = jnp.where(lane == line + width, 1.0, work)
    for k in range(rank):
        top = 8 * (k // 8)
        column = columns[k]
        inverse_root = lax.rsqrt(column[k - top : k - top + 1])
        column = column * inverse_root
        for j in range(k + 1, rank):
            first = 8 * (j // 8) - top
            columns[j] = columns[j] - column[first:] * column[j - top : j - top + 1]
        row = work[k : k + 1] * inverse_root
        rest = work[top:] - jnp.where(line[top:] > k, column, 0.0) * row
        rest = jnp.where(line[top:] == k, row, rest)
        work = jnp.concatenate([work[:top], rest], axis=0) if top else rest
    return work[:, width : width + rank], work[:, :width]


def factor_kernel(got_ref, next_ref, mix_ref, norm_ref, share_ref):
    rank, width = next_ref.shape
    half = rank // 2
    peers, _, chunk = got_ref.shape
    share = share_ref.shape[0]
    for peer in range(peers):
        mine = got_ref[peer, half:rank, 3 * rank :].astype(F32)
        mine = jnp.concatenate([mine[i : i + share] for i in range(0, half, share)], axis=1)
        share_ref[:, peer * chunk : (peer + 1) * chunk] = mine.astype(BF16)
    sums = [got_ref[peer].astype(F32) for peer in range(peers)]
    while len(sums) > 1:
        sums = [sum(sums[i + 1 : i + 2], sums[i]) for i in range(0, len(sums), 2)]
    upper, lower = sums[0][:half], sums[0][half:]
    upper = upper[:, : 2 * width] + upper[:, 2 * width :]
    product = jnp.concatenate([upper[:, :width], upper[:, width:]], axis=0)
    third = jnp.concatenate(
        [lower[:, 2 * rank + 2 : 3 * rank], jnp.zeros((half, 3), F32)], axis=1
    )
    gram = unpack_gram(lower[:, : rank + 1] + lower[:, rank + 1 : 2 * rank + 2] + third)
    line = lax.broadcasted_iota(jnp.int32, (rank, rank), 0)
    eye = (line == lax.broadcasted_iota(jnp.int32, (rank, rank), 1)).astype(F32)
    trace = jnp.sum(gram * eye)
    inverse, next_factor = eliminate(gram + (0.0001 * trace / rank) * eye, product)
    next_ref[...] = next_factor
    norm_ref[...] = jnp.full(norm_ref.shape, jnp.sum(next_factor * next_factor), F32)
    mix = lax.dot_general(
        next_factor,
        inverse,
        (((0,), (0,)), ((), ())),
        precision=HIGHEST,
        preferred_element_type=F32,
    )
    mix_ref[...] = jnp.concatenate(
        [*split(mix, 3), jnp.zeros((width, LANES - 3 * rank), BF16)], axis=1
    )


def update_kernel(
    norm_limit, norms_ref, shares_ref, mix_ref, gradient_ref, error_ref, applied_ref, next_ref, applied_tile, next_tile, sems
):
    width, row_count = next_ref.shape
    rank = shares_ref.shape[0] * shares_ref.shape[1]
    mix = mix_ref[...][:, : 3 * rank]
    norm_sq = jnp.sum(norms_ref[...][:, 0:1], axis=0, keepdims=True)
    clip_scale = jnp.minimum(1.0, norm_limit * lax.rsqrt(norm_sq + 1e-06))
    pieces = sems.shape[0]
    span = row_count // pieces
    step = min(512, span)
    puts = []
    for piece in range(pieces):
        for start in range(piece * span, (piece + 1) * span, step):
            part = slice(start, start + step)
            rows = jnp.concatenate(
                [shares_ref[i, :, part].astype(F32) for i in range(shares_ref.shape[0])], axis=0
            ).astype(BF16)
            decompressed = jnp.dot(
                mix, jnp.concatenate([rows, rows, rows], axis=0), preferred_element_type=F32
            )
            applied_tile[:, part] = (clip_scale * decompressed).astype(BF16)
            tile = (gradient_ref[:, part].astype(F32) + error_ref[:, part].astype(F32)).astype(BF16)
            next_tile[:, part] = (tile.astype(F32) - decompressed).astype(BF16)
        part = pl.ds(piece * span, span)
        for i, (source, target) in enumerate(((applied_tile, applied_ref), (next_tile, next_ref))):
            put = pltpu.make_async_copy(source.at[:, part], target.at[:, part], sems.at[piece, i])
            put.start()
            puts.append(put)
    for put in puts:
        put.wait()


def call(kernel, outs, *args, vmem=16, spaces=None, out_space=pltpu.VMEM, scratch=(), cost=None):
    spaces = spaces or [pltpu.VMEM] * len(args)
    return pl.pallas_call(
        kernel,
        out_shape=outs,
        in_specs=[pl.BlockSpec(memory_space=space) for space in spaces],
        out_specs=jax.tree.map(lambda _: pl.BlockSpec(memory_space=out_space), outs),
        scratch_shapes=scratch,
        compiler_params=pltpu.CompilerParams(vmem_limit_bytes=vmem * 1024 * 1024),
        cost_estimate=cost,
    )(*args)


def per_device(gradient, error_buffer, warm_factor):
    shape = jax.ShapeDtypeStruct
    replicas, far, near, groups = (lax.axis_size(axis) for axis in ("gx", "far", "near", "gz"))
    plane, groups, columns = ("gx", "near", "gz"), near * groups, far * near * groups
    gradient, error_buffer = gradient[0], error_buffer[0]
    width, row_count = gradient.shape
    rank = warm_factor.shape[0]
    peers = replicas * groups
    chunk = row_count // peers
    norm_limit = 0.1 * math.sqrt(width * columns * row_count)
    pieces = min(4, peers)
    message = shape((peers, (width * chunk + rank * width) // LANES, LANES), BF16)

    send = call(
        merge_kernel,
        message,
        *(
            pltpu.with_memory_space_constraint(x, pltpu.HBM)
            for x in (gradient, error_buffer, warm_factor)
        ),
        spaces=[pltpu.HBM] * 3,
        scratch=[
            pltpu.VMEM((width, row_count), BF16),
            pltpu.VMEM((width, row_count), BF16),
            pltpu.VMEM((rank, width), F32),
            pltpu.SemaphoreType.DMA((pieces, 3)),
        ],
    )
    got = lax.all_to_all(send, plane, 0, 0)
    mean, send = call(
        lambda *refs: rows_kernel(groups, width, 1.0 / replicas, *refs),
        (shape((groups * width, chunk), F32), shape((far, rank, chunk), BF16)),
        got,
    )
    got = lax.all_to_all(send, "far", 0, 0)
    message = shape((peers, rank, LANES), BF16)
    send = call(lambda *refs: columns_kernel(groups, *refs), message, got, mean)
    got = lax.all_to_all(send, plane, 0, 0)
    next_factor, mix, norm, share = call(
        factor_kernel,
        (
            shape((rank, width), F32),
            shape((width, LANES), BF16),
            shape((columns, LANES), F32),
            shape((rank // replicas, row_count), BF16),
        ),
        got,
    )
    norms = lax.all_to_all(norm, ("far", "near", "gz"), 0, 0, tiled=True)
    shares = lax.all_gather(share, "gx")
    applied, next_error = call(
        lambda *refs: update_kernel(norm_limit, *refs),
        (shape((width, row_count), BF16), shape((width, row_count), BF16)),
        norms,
        shares,
        mix,
        gradient,
        error_buffer,
        out_space=pl.ANY,
        scratch=[
            pltpu.VMEM((width, row_count), BF16),
            pltpu.VMEM((width, row_count), BF16),
            pltpu.SemaphoreType.DMA((8, 2)),
        ],
    )
    return applied, next_error[None], next_factor


def solution(mesh):
    replicas, depth, groups = (mesh.shape[axis] for axis in ("gx", "gy", "gz"))
    near = math.gcd(depth, 2)
    fine = jax.sharding.Mesh(
        mesh.devices.reshape(replicas, depth // near, near, groups), ("gx", "far", "near", "gz")
    )
    columns = ("far", "near", "gz")
    in_specs = (P("gx", columns, None), P("gx", columns, None), P(None, columns))
    out_specs = (P(columns, None), P("gx", columns, None), P(None, columns))
    return jax.shard_map(
        per_device, mesh=fine, in_specs=in_specs, out_specs=out_specs, check_vma=False
    )
```

```python
import math

import jax
import jax.numpy as jnp
from jax import lax
from jax.experimental import pallas as pl
from jax.experimental.pallas import tpu as pltpu
from jax.sharding import PartitionSpec as P

F32 = jnp.float32
BF16 = jnp.bfloat16
HIGHEST = lax.Precision.HIGHEST
LANES = 128


def split(value, pieces):
    parts = []
    for _ in range(pieces):
        part = value.astype(BF16)
        parts.append(part)
        value = value - part.astype(F32)
    return parts


def merge_kernel(gradient_ref, error_ref, warm_ref, send_ref, gradient_tile, error_tile, warm_tile, sems):
    peers, tall, _ = send_ref.shape
    width, row_count = gradient_ref.shape
    chunk = row_count // peers
    rank = warm_ref.shape[0]
    extra = rank * width // LANES
    pieces = sems.shape[0]
    per_piece = peers // pieces
    gets = []
    for piece in range(pieces):
        part = pl.ds(piece * per_piece * chunk, per_piece * chunk)
        gets.append(
            (
                pltpu.make_async_copy(gradient_ref.at[:, part], gradient_tile.at[:, part], sems.at[piece, 0]),
                pltpu.make_async_copy(error_ref.at[:, part], error_tile.at[:, part], sems.at[piece, 1]),
            )
        )
    warm_get = pltpu.make_async_copy(warm_ref, warm_tile, sems.at[0, 2])
    warm_get.start()
    for pair in gets:
        pair[0].start()
        pair[1].start()
    warm_get.wait()
    packed = jnp.concatenate(
        [warm_tile[i : i + extra] for i in range(0, rank, extra)], axis=1
    ).astype(BF16)
    for piece in range(pieces):
        gets[piece][0].wait()
        gets[piece][1].wait()
        for peer in range(piece * per_piece, (piece + 1) * per_piece):
            for i in range(chunk // LANES):
                part = slice(peer * chunk + i * LANES, peer * chunk + (i + 1) * LANES)
                tile = gradient_tile[:, part].astype(F32) + error_tile[:, part].astype(F32)
                send_ref[peer, i * width : (i + 1) * width, :] = tile.astype(BF16)
            send_ref[peer, tall - extra :, :] = packed


def rows_kernel(groups, width, scale, got_ref, mean_ref, send_ref):
    peers, tall, _ = got_ref.shape
    chunk = mean_ref.shape[1]
    high = width * chunk // LANES
    replicas = peers // groups
    warm = []
    for group in range(groups):
        total = got_ref[group, 0:high, :].astype(F32)
        for replica in range(1, replicas):
            total += got_ref[replica * groups + group, 0:high, :].astype(F32)
        total *= scale
        for i in range(chunk // LANES):
            mean_ref[group * width : (group + 1) * width, i * LANES : (i + 1) * LANES] = total[
                i * width : (i + 1) * width
            ]
        packed = got_ref[group, high:, :].astype(F32)
        warm.append(
            jnp.concatenate([packed[:, i : i + width] for i in range(0, LANES, width)], axis=0)
        )
    rows = jnp.dot(
        jnp.concatenate(warm, axis=1), mean_ref[...], precision=HIGHEST, preferred_element_type=F32
    ).astype(BF16)
    for peer in range(send_ref.shape[0]):
        send_ref[peer] = rows


def add(got_ref):
    total = got_ref[0].astype(F32)
    for peer in range(1, got_ref.shape[0]):
        total += got_ref[peer].astype(F32)
    return total.astype(BF16)


def pack_gram(gram):
    half = gram.shape[0] // 2
    first, cross, second = gram[:half, :half], gram[:half, half:], gram[half:, half:]
    line = lax.broadcasted_iota(jnp.int32, (half, half), 0)
    lane = lax.broadcasted_iota(jnp.int32, (half, half), 1)
    diagonal = jnp.sum(jnp.where(line == lane, second, 0.0), axis=1, keepdims=True)
    return jnp.concatenate([jnp.where(line <= lane, first, second), diagonal, cross], axis=1)


def unpack_gram(packed):
    half = packed.shape[0]
    line = lax.broadcasted_iota(jnp.int32, (half, half), 0)
    lane = lax.broadcasted_iota(jnp.int32, (half, half), 1)
    both, diagonal, cross = packed[:, :half], packed[:, half : half + 1], packed[:, half + 1 :]
    first = jnp.where(line <= lane, both, 0.0)
    second = jnp.where(line > lane, both, jnp.where(line == lane, diagonal, 0.0))
    once = jnp.concatenate(
        [
            jnp.concatenate([first, cross], axis=1),
            jnp.concatenate([jnp.zeros((half, half), F32), second], axis=1),
        ],
        axis=0,
    )
    line = lax.broadcasted_iota(jnp.int32, (2 * half, 2 * half), 0)
    eye = line == lax.broadcasted_iota(jnp.int32, (2 * half, 2 * half), 1)
    return jnp.where(eye, once, once + once.T)


def columns_kernel(groups, got_ref, mean_ref, send_ref):
    rank, chunk = got_ref.shape[1:]
    half = rank // 2
    replicas = send_ref.shape[0] // groups
    rows = add(got_ref)
    across = (((1,), (1,)), ((), ()))
    product = lax.dot_general(
        rows.astype(F32), mean_ref[...], across, precision=HIGHEST, preferred_element_type=F32
    )
    gram = lax.dot_general(rows, rows, across, preferred_element_type=F32)
    pieces = jnp.concatenate(split(pack_gram(gram), 3), axis=1)[:, : 3 * rank].astype(F32)
    rows = rows.astype(F32)
    share, block = rank // replicas, chunk // (half * replicas // rank)
    lower = []
    for replica in range(replicas):
        mine = rows[replica * share : (replica + 1) * share]
        mine = jnp.concatenate([mine[:, i : i + block] for i in range(0, chunk, block)], axis=0)
        lower.append(jnp.concatenate([pieces, mine], axis=1).astype(BF16))
    width = product.shape[1] // groups
    for group in range(groups):
        high, low = split(product[:, group * width : (group + 1) * width], 2)
        upper = jnp.concatenate([high[:half], high[half:], low[:half], low[half:]], axis=1)
        for replica in range(replicas):
            peer = replica * groups + group
            send_ref[peer, 0:half, :] = upper
            send_ref[peer, half:rank, :] = lower[replica]


def eliminate(gram, product):
    rank, width = product.shape
    columns = [
        jnp.broadcast_to(gram[8 * (j // 8) :, j : j + 1], (rank - 8 * (j // 8), LANES))
        for j in range(rank)
    ]
    line = lax.broadcasted_iota(jnp.int32, (rank, LANES), 0)
    lane = lax.broadcasted_iota(jnp.int32, (rank, LANES), 1)
    work = jnp.concatenate([product, jnp.zeros((rank, LANES - width), F32)], axis=1)
    work = jnp.where(lane == line + width, 1.0, work)
    for k in range(rank):
        top = 8 * (k // 8)
        column = columns[k]
        inverse_root = lax.rsqrt(column[k - top : k - top + 1])
        column = column * inverse_root
        for j in range(k + 1, rank):
            first = 8 * (j // 8) - top
            columns[j] = columns[j] - column[first:] * column[j - top : j - top + 1]
        row = work[k : k + 1] * inverse_root
        rest = work[top:] - jnp.where(line[top:] > k, column, 0.0) * row
        rest = jnp.where(line[top:] == k, row, rest)
        work = jnp.concatenate([work[:top], rest], axis=0) if top else rest
    return work[:, width : width + rank], work[:, :width]


def factor_kernel(
    got_ref, next_ref, norm_ref, mix_ref, share_ref, next_tile, norm_tile, sems
):
    rank, width = next_ref.shape
    half = rank // 2
    peers, _, chunk = got_ref.shape
    share = share_ref.shape[0]
    sums = [got_ref[peer].astype(F32) for peer in range(peers)]
    while len(sums) > 1:
        sums = [sum(sums[i + 1 : i + 2], sums[i]) for i in range(0, len(sums), 2)]
    upper, lower = sums[0][:half], sums[0][half:]
    upper = upper[:, : 2 * width] + upper[:, 2 * width :]
    product = jnp.concatenate([upper[:, :width], upper[:, width:]], axis=0)
    third = jnp.concatenate(
        [lower[:, 2 * rank + 2 : 3 * rank], jnp.zeros((half, 3), F32)], axis=1
    )
    gram = unpack_gram(lower[:, : rank + 1] + lower[:, rank + 1 : 2 * rank + 2] + third)
    line = lax.broadcasted_iota(jnp.int32, (rank, rank), 0)
    eye = (line == lax.broadcasted_iota(jnp.int32, (rank, rank), 1)).astype(F32)
    trace = jnp.sum(gram * eye)
    inverse, next_factor = eliminate(gram + (0.0001 * trace / rank) * eye, product)
    norm_tile[...] = jnp.full(norm_tile.shape, jnp.sum(next_factor * next_factor), F32)
    norm_put = pltpu.make_async_copy(norm_tile, norm_ref, sems.at[0])
    norm_put.start()
    next_tile[...] = next_factor
    next_put = pltpu.make_async_copy(next_tile, next_ref, sems.at[1])
    next_put.start()
    mix = lax.dot_general(
        next_factor,
        inverse,
        (((0,), (0,)), ((), ())),
        precision=HIGHEST,
        preferred_element_type=F32,
    )
    mix_ref[...] = jnp.concatenate(
        [*split(mix, 3), jnp.zeros((width, LANES - 3 * rank), BF16)], axis=1
    )
    for peer in range(peers):
        mine = got_ref[peer, half:rank, 3 * rank :].astype(F32)
        mine = jnp.concatenate([mine[i : i + share] for i in range(0, half, share)], axis=1)
        share_ref[:, peer * chunk : (peer + 1) * chunk] = mine.astype(BF16)
    norm_put.wait()
    next_put.wait()


def update_kernel(
    norm_limit, norms_ref, shares_ref, mix_ref, gradient_ref, error_ref, applied_ref, next_ref, applied_tile, next_tile, sems
):
    width, row_count = next_ref.shape
    rank = shares_ref.shape[0] * shares_ref.shape[1]
    mix = mix_ref[...][:, : 3 * rank]
    norm_sq = jnp.sum(norms_ref[...][:, 0:1], axis=0, keepdims=True)
    clip_scale = jnp.minimum(1.0, norm_limit * lax.rsqrt(norm_sq + 1e-06))
    pieces = sems.shape[0]
    span = row_count // pieces
    step = min(512, span)
    puts = []
    for piece in range(pieces):
        for start in range(piece * span, (piece + 1) * span, step):
            part = slice(start, start + step)
            rows = jnp.concatenate(
                [shares_ref[i, :, part].astype(F32) for i in range(shares_ref.shape[0])], axis=0
            ).astype(BF16)
            decompressed = jnp.dot(
                mix, jnp.concatenate([rows, rows, rows], axis=0), preferred_element_type=F32
            )
            applied_tile[:, part] = (clip_scale * decompressed).astype(BF16)
            tile = (gradient_ref[:, part].astype(F32) + error_ref[:, part].astype(F32)).astype(BF16)
            next_tile[:, part] = (tile.astype(F32) - decompressed).astype(BF16)
        part = pl.ds(piece * span, span)
        for i, (source, target) in enumerate(((applied_tile, applied_ref), (next_tile, next_ref))):
            put = pltpu.make_async_copy(source.at[:, part], target.at[:, part], sems.at[piece, i])
            put.start()
            puts.append(put)
    for put in puts:
        put.wait()


def call(kernel, outs, *args, vmem=16, spaces=None, out_space=pltpu.VMEM, scratch=(), cost=None):
    spaces = spaces or [pltpu.VMEM] * len(args)
    return pl.pallas_call(
        kernel,
        out_shape=outs,
        in_specs=[pl.BlockSpec(memory_space=space) for space in spaces],
        out_specs=jax.tree.map(lambda space: pl.BlockSpec(memory_space=space), out_space)
        if isinstance(out_space, tuple)
        else jax.tree.map(lambda _: pl.BlockSpec(memory_space=out_space), outs),
        scratch_shapes=scratch,
        compiler_params=pltpu.CompilerParams(vmem_limit_bytes=vmem * 1024 * 1024),
        cost_estimate=cost,
    )(*args)


def per_device(gradient, error_buffer, warm_factor):
    shape = jax.ShapeDtypeStruct
    replicas, far, near, groups = (lax.axis_size(axis) for axis in ("gx", "far", "near", "gz"))
    plane, groups, columns = ("gx", "near", "gz"), near * groups, far * near * groups
    gradient, error_buffer = gradient[0], error_buffer[0]
    width, row_count = gradient.shape
    rank = warm_factor.shape[0]
    peers = replicas * groups
    chunk = row_count // peers
    norm_limit = 0.1 * math.sqrt(width * columns * row_count)
    pieces = min(4, peers)
    message = shape((peers, (width * chunk + rank * width) // LANES, LANES), BF16)

    send = call(
        merge_kernel,
        message,
        *(
            pltpu.with_memory_space_constraint(x, pltpu.HBM)
            for x in (gradient, error_buffer, warm_factor)
        ),
        spaces=[pltpu.HBM] * 3,
        scratch=[
            pltpu.VMEM((width, row_count), BF16),
            pltpu.VMEM((width, row_count), BF16),
            pltpu.VMEM((rank, width), F32),
            pltpu.SemaphoreType.DMA((pieces, 3)),
        ],
    )
    got = lax.all_to_all(send, plane, 0, 0)
    mean, send = call(
        lambda *refs: rows_kernel(groups, width, 1.0 / replicas, *refs),
        (shape((groups * width, chunk), F32), shape((far, rank, chunk), BF16)),
        got,
    )
    got = lax.all_to_all(send, "far", 0, 0)
    message = shape((peers, rank, LANES), BF16)
    send = call(lambda *refs: columns_kernel(groups, *refs), message, got, mean)
    got = lax.all_to_all(send, plane, 0, 0)
    next_factor, norm, mix, share = call(
        factor_kernel,
        (
            shape((rank, width), F32),
            shape((columns, LANES), F32),
            shape((width, LANES), BF16),
            shape((rank // replicas, row_count), BF16),
        ),
        got,
        out_space=(pl.ANY, pl.ANY, pltpu.VMEM, pltpu.VMEM),
        scratch=[
            pltpu.VMEM((rank, width), F32),
            pltpu.VMEM((columns, LANES), F32),
            pltpu.SemaphoreType.DMA((2,)),
        ],
    )
    norms = lax.all_to_all(norm, ("far", "near", "gz"), 0, 0, tiled=True)
    shares = lax.all_gather(share, "gx")
    applied, next_error = call(
        lambda *refs: update_kernel(norm_limit, *refs),
        (shape((width, row_count), BF16), shape((width, row_count), BF16)),
        norms,
        shares,
        mix,
        gradient,
        error_buffer,
        out_space=pl.ANY,
        scratch=[
            pltpu.VMEM((width, row_count), BF16),
            pltpu.VMEM((width, row_count), BF16),
            pltpu.SemaphoreType.DMA((8, 2)),
        ],
    )
    return applied, next_error[None], next_factor


def solution(mesh):
    replicas, depth, groups = (mesh.shape[axis] for axis in ("gx", "gy", "gz"))
    near = math.gcd(depth, 2)
    fine = jax.sharding.Mesh(
        mesh.devices.reshape(replicas, depth // near, near, groups), ("gx", "far", "near", "gz")
    )
    columns = ("far", "near", "gz")
    in_specs = (P("gx", columns, None), P("gx", columns, None), P(None, columns))
    out_specs = (P(columns, None), P("gx", columns, None), P(None, columns))
    return jax.shard_map(
        per_device, mesh=fine, in_specs=in_specs, out_specs=out_specs, check_vma=False
    )
```

```python
import math

import jax
import jax.numpy as jnp
from jax import lax
from jax.experimental import pallas as pl
from jax.experimental.pallas import tpu as pltpu
from jax.sharding import PartitionSpec as P

F32 = jnp.float32
BF16 = jnp.bfloat16
HIGHEST = lax.Precision.HIGHEST
LANES = 128


def split(value, pieces):
    parts = []
    for _ in range(pieces):
        part = value.astype(BF16)
        parts.append(part)
        value = value - part.astype(F32)
    return parts


def merge_kernel(gradient_ref, error_ref, warm_ref, send_ref, gradient_tile, error_tile, warm_tile, sems):
    peers, tall, _ = send_ref.shape
    width, row_count = gradient_ref.shape
    chunk = row_count // peers
    rank = warm_ref.shape[0]
    extra = rank * width // LANES
    pieces = sems.shape[0]
    per_piece = peers // pieces
    gets = []
    for piece in range(pieces):
        part = pl.ds(piece * per_piece * chunk, per_piece * chunk)
        gets.append(
            (
                pltpu.make_async_copy(gradient_ref.at[:, part], gradient_tile.at[:, part], sems.at[piece, 0]),
                pltpu.make_async_copy(error_ref.at[:, part], error_tile.at[:, part], sems.at[piece, 1]),
            )
        )
    warm_get = pltpu.make_async_copy(warm_ref, warm_tile, sems.at[0, 2])
    warm_get.start()
    for pair in gets:
        pair[0].start()
        pair[1].start()
    warm_get.wait()
    packed = jnp.concatenate(
        [warm_tile[i : i + extra] for i in range(0, rank, extra)], axis=1
    ).astype(BF16)
    for piece in range(pieces):
        gets[piece][0].wait()
        gets[piece][1].wait()
        for peer in range(piece * per_piece, (piece + 1) * per_piece):
            for i in range(chunk // LANES):
                part = slice(peer * chunk + i * LANES, peer * chunk + (i + 1) * LANES)
                tile = gradient_tile[:, part].astype(F32) + error_tile[:, part].astype(F32)
                send_ref[peer, i * width : (i + 1) * width, :] = tile.astype(BF16)
            send_ref[peer, tall - extra :, :] = packed


def rows_kernel(groups, width, scale, got_ref, mean_ref, send_ref):
    peers, tall, _ = got_ref.shape
    chunk = mean_ref.shape[1]
    high = width * chunk // LANES
    replicas = peers // groups
    warm = []
    for group in range(groups):
        total = got_ref[group, 0:high, :].astype(F32)
        for replica in range(1, replicas):
            total += got_ref[replica * groups + group, 0:high, :].astype(F32)
        total *= scale
        for i in range(chunk // LANES):
            mean_ref[group * width : (group + 1) * width, i * LANES : (i + 1) * LANES] = total[
                i * width : (i + 1) * width
            ]
        packed = got_ref[group, high:, :].astype(F32)
        warm.append(
            jnp.concatenate([packed[:, i : i + width] for i in range(0, LANES, width)], axis=0)
        )
    warm = jnp.concatenate(warm, axis=1).astype(BF16)
    rows = sum(
        jnp.dot(warm, piece, preferred_element_type=F32) for piece in split(mean_ref[...], 3)
    ).astype(BF16)
    for peer in range(send_ref.shape[0]):
        send_ref[peer] = rows


def add(got_ref):
    total = got_ref[0].astype(F32)
    for peer in range(1, got_ref.shape[0]):
        total += got_ref[peer].astype(F32)
    return total.astype(BF16)


def pack_gram(gram):
    half = gram.shape[0] // 2
    first, cross, second = gram[:half, :half], gram[:half, half:], gram[half:, half:]
    line = lax.broadcasted_iota(jnp.int32, (half, half), 0)
    lane = lax.broadcasted_iota(jnp.int32, (half, half), 1)
    diagonal = jnp.sum(jnp.where(line == lane, second, 0.0), axis=1, keepdims=True)
    return jnp.concatenate([jnp.where(line <= lane, first, second), diagonal, cross], axis=1)


def unpack_gram(packed):
    half = packed.shape[0]
    line = lax.broadcasted_iota(jnp.int32, (half, half), 0)
    lane = lax.broadcasted_iota(jnp.int32, (half, half), 1)
    both, diagonal, cross = packed[:, :half], packed[:, half : half + 1], packed[:, half + 1 :]
    first = jnp.where(line <= lane, both, 0.0)
    second = jnp.where(line > lane, both, jnp.where(line == lane, diagonal, 0.0))
    once = jnp.concatenate(
        [
            jnp.concatenate([first, cross], axis=1),
            jnp.concatenate([jnp.zeros((half, half), F32), second], axis=1),
        ],
        axis=0,
    )
    line = lax.broadcasted_iota(jnp.int32, (2 * half, 2 * half), 0)
    eye = line == lax.broadcasted_iota(jnp.int32, (2 * half, 2 * half), 1)
    return jnp.where(eye, once, once + once.T)


def columns_kernel(groups, got_ref, mean_ref, send_ref):
    rank, chunk = got_ref.shape[1:]
    half = rank // 2
    replicas = send_ref.shape[0] // groups
    rows = add(got_ref)
    across = (((1,), (1,)), ((), ()))
    product = sum(
        lax.dot_general(rows, piece, across, preferred_element_type=F32)
        for piece in split(mean_ref[...], 3)
    )
    gram = lax.dot_general(rows, rows, across, preferred_element_type=F32)
    pieces = jnp.concatenate(split(pack_gram(gram), 3), axis=1)[:, : 3 * rank].astype(F32)
    rows = rows.astype(F32)
    share, block = rank // replicas, chunk // (half * replicas // rank)
    lower = []
    for replica in range(replicas):
        mine = rows[replica * share : (replica + 1) * share]
        mine = jnp.concatenate([mine[:, i : i + block] for i in range(0, chunk, block)], axis=0)
        lower.append(jnp.concatenate([pieces, mine], axis=1).astype(BF16))
    width = product.shape[1] // groups
    for group in range(groups):
        high, low = split(product[:, group * width : (group + 1) * width], 2)
        upper = jnp.concatenate([high[:half], high[half:], low[:half], low[half:]], axis=1)
        for replica in range(replicas):
            peer = replica * groups + group
            send_ref[peer, 0:half, :] = upper
            send_ref[peer, half:rank, :] = lower[replica]


def eliminate(gram, product):
    rank, width = product.shape
    columns = [
        jnp.broadcast_to(gram[8 * (j // 8) :, j : j + 1], (rank - 8 * (j // 8), LANES))
        for j in range(rank)
    ]
    line = lax.broadcasted_iota(jnp.int32, (rank, LANES), 0)
    lane = lax.broadcasted_iota(jnp.int32, (rank, LANES), 1)
    work = jnp.concatenate([product, jnp.zeros((rank, LANES - width), F32)], axis=1)
    work = jnp.where(lane == line + width, 1.0, work)
    for k in range(rank):
        top = 8 * (k // 8)
        column = columns[k]
        inverse_root = lax.rsqrt(column[k - top : k - top + 1])
        column = column * inverse_root
        for j in range(k + 1, rank):
            first = 8 * (j // 8) - top
            columns[j] = columns[j] - column[first:] * column[j - top : j - top + 1]
        row = work[k : k + 1] * inverse_root
        rest = work[top:] - jnp.where(line[top:] > k, column, 0.0) * row
        rest = jnp.where(line[top:] == k, row, rest)
        work = jnp.concatenate([work[:top], rest], axis=0) if top else rest
    return work[:, width : width + rank], work[:, :width]


def factor_kernel(got_ref, next_ref, mix_ref, norm_ref, share_ref):
    rank, width = next_ref.shape
    half = rank // 2
    peers, _, chunk = got_ref.shape
    share = share_ref.shape[0]
    for peer in range(peers):
        mine = got_ref[peer, half:rank, 3 * rank :].astype(F32)
        mine = jnp.concatenate([mine[i : i + share] for i in range(0, half, share)], axis=1)
        share_ref[:, peer * chunk : (peer + 1) * chunk] = mine.astype(BF16)
    sums = [got_ref[peer].astype(F32) for peer in range(peers)]
    while len(sums) > 1:
        sums = [sum(sums[i + 1 : i + 2], sums[i]) for i in range(0, len(sums), 2)]
    upper, lower = sums[0][:half], sums[0][half:]
    upper = upper[:, : 2 * width] + upper[:, 2 * width :]
    product = jnp.concatenate([upper[:, :width], upper[:, width:]], axis=0)
    third = jnp.concatenate(
        [lower[:, 2 * rank + 2 : 3 * rank], jnp.zeros((half, 3), F32)], axis=1
    )
    gram = unpack_gram(lower[:, : rank + 1] + lower[:, rank + 1 : 2 * rank + 2] + third)
    line = lax.broadcasted_iota(jnp.int32, (rank, rank), 0)
    eye = (line == lax.broadcasted_iota(jnp.int32, (rank, rank), 1)).astype(F32)
    trace = jnp.sum(gram * eye)
    inverse, next_factor = eliminate(gram + (0.0001 * trace / rank) * eye, product)
    next_ref[...] = next_factor
    norm_ref[...] = jnp.full(norm_ref.shape, jnp.sum(next_factor * next_factor), F32)
    mix = lax.dot_general(
        next_factor,
        inverse,
        (((0,), (0,)), ((), ())),
        precision=HIGHEST,
        preferred_element_type=F32,
    )
    mix_ref[...] = jnp.concatenate(
        [*split(mix, 3), jnp.zeros((width, LANES - 3 * rank), BF16)], axis=1
    )


def update_kernel(
    norm_limit, norms_ref, shares_ref, mix_ref, gradient_ref, error_ref, applied_ref, next_ref, applied_tile, next_tile, sems
):
    width, row_count = next_ref.shape
    rank = shares_ref.shape[0] * shares_ref.shape[1]
    mix = mix_ref[...][:, : 3 * rank]
    norm_sq = jnp.sum(norms_ref[...][:, 0:1], axis=0, keepdims=True)
    clip_scale = jnp.minimum(1.0, norm_limit * lax.rsqrt(norm_sq + 1e-06))
    pieces = sems.shape[0]
    span = row_count // pieces
    step = min(512, span)
    puts = []
    for piece in range(pieces):
        for start in range(piece * span, (piece + 1) * span, step):
            part = slice(start, start + step)
            rows = jnp.concatenate(
                [shares_ref[i, :, part].astype(F32) for i in range(shares_ref.shape[0])], axis=0
            ).astype(BF16)
            decompressed = jnp.dot(
                mix, jnp.concatenate([rows, rows, rows], axis=0), preferred_element_type=F32
            )
            applied_tile[:, part] = (clip_scale * decompressed).astype(BF16)
            tile = (gradient_ref[:, part].astype(F32) + error_ref[:, part].astype(F32)).astype(BF16)
            next_tile[:, part] = (tile.astype(F32) - decompressed).astype(BF16)
        part = pl.ds(piece * span, span)
        for i, (source, target) in enumerate(((applied_tile, applied_ref), (next_tile, next_ref))):
            put = pltpu.make_async_copy(source.at[:, part], target.at[:, part], sems.at[piece, i])
            put.start()
            puts.append(put)
    for put in puts:
        put.wait()


def call(kernel, outs, *args, vmem=16, spaces=None, out_space=pltpu.VMEM, scratch=(), cost=None):
    spaces = spaces or [pltpu.VMEM] * len(args)
    return pl.pallas_call(
        kernel,
        out_shape=outs,
        in_specs=[pl.BlockSpec(memory_space=space) for space in spaces],
        out_specs=jax.tree.map(lambda _: pl.BlockSpec(memory_space=out_space), outs),
        scratch_shapes=scratch,
        compiler_params=pltpu.CompilerParams(vmem_limit_bytes=vmem * 1024 * 1024),
        cost_estimate=cost,
    )(*args)


def per_device(gradient, error_buffer, warm_factor):
    shape = jax.ShapeDtypeStruct
    replicas, far, near, groups = (lax.axis_size(axis) for axis in ("gx", "far", "near", "gz"))
    plane, groups, columns = ("gx", "near", "gz"), near * groups, far * near * groups
    gradient, error_buffer = gradient[0], error_buffer[0]
    width, row_count = gradient.shape
    rank = warm_factor.shape[0]
    peers = replicas * groups
    chunk = row_count // peers
    norm_limit = 0.1 * math.sqrt(width * columns * row_count)
    pieces = min(4, peers)
    message = shape((peers, (width * chunk + rank * width) // LANES, LANES), BF16)

    send = call(
        merge_kernel,
        message,
        *(
            pltpu.with_memory_space_constraint(x, pltpu.HBM)
            for x in (gradient, error_buffer, warm_factor)
        ),
        spaces=[pltpu.HBM] * 3,
        scratch=[
            pltpu.VMEM((width, row_count), BF16),
            pltpu.VMEM((width, row_count), BF16),
            pltpu.VMEM((rank, width), F32),
            pltpu.SemaphoreType.DMA((pieces, 3)),
        ],
    )
    got = lax.all_to_all(send, plane, 0, 0)
    mean, send = call(
        lambda *refs: rows_kernel(groups, width, 1.0 / replicas, *refs),
        (shape((groups * width, chunk), F32), shape((far, rank, chunk), BF16)),
        got,
    )
    got = lax.all_to_all(send, "far", 0, 0)
    message = shape((peers, rank, LANES), BF16)
    send = call(lambda *refs: columns_kernel(groups, *refs), message, got, mean)
    got = lax.all_to_all(send, plane, 0, 0)
    next_factor, mix, norm, share = call(
        factor_kernel,
        (
            shape((rank, width), F32),
            shape((width, LANES), BF16),
            shape((columns, LANES), F32),
            shape((rank // replicas, row_count), BF16),
        ),
        got,
    )
    norms = lax.all_to_all(norm, ("far", "near", "gz"), 0, 0, tiled=True)
    shares = lax.all_gather(share, "gx")
    applied, next_error = call(
        lambda *refs: update_kernel(norm_limit, *refs),
        (shape((width, row_count), BF16), shape((width, row_count), BF16)),
        norms,
        shares,
        mix,
        gradient,
        error_buffer,
        out_space=pl.ANY,
        scratch=[
            pltpu.VMEM((width, row_count), BF16),
            pltpu.VMEM((width, row_count), BF16),
            pltpu.SemaphoreType.DMA((8, 2)),
        ],
    )
    return applied, next_error[None], next_factor


def solution(mesh):
    replicas, depth, groups = (mesh.shape[axis] for axis in ("gx", "gy", "gz"))
    near = math.gcd(depth, 2)
    fine = jax.sharding.Mesh(
        mesh.devices.reshape(replicas, depth // near, near, groups), ("gx", "far", "near", "gz")
    )
    columns = ("far", "near", "gz")
    in_specs = (P("gx", columns, None), P("gx", columns, None), P(None, columns))
    out_specs = (P(columns, None), P("gx", columns, None), P(None, columns))
    return jax.shard_map(
        per_device, mesh=fine, in_specs=in_specs, out_specs=out_specs, check_vma=False
    )
```

```python
import math

import jax
import jax.numpy as jnp
from jax import lax
from jax.experimental import pallas as pl
from jax.experimental.pallas import tpu as pltpu
from jax.sharding import PartitionSpec as P

F32 = jnp.float32
BF16 = jnp.bfloat16
HIGHEST = lax.Precision.HIGHEST
LANES = 128


def split(value, pieces):
    parts = []
    for _ in range(pieces):
        part = value.astype(BF16)
        parts.append(part)
        value = value - part.astype(F32)
    return parts


def merge_kernel(gradient_ref, error_ref, warm_ref, send_ref, gradient_tile, error_tile, warm_tile, sems):
    peers, tall, _ = send_ref.shape
    width, row_count = gradient_ref.shape
    chunk = row_count // peers
    rank = warm_ref.shape[0]
    extra = rank * width // LANES
    pieces = sems.shape[0]
    per_piece = peers // pieces
    gets = []
    for piece in range(pieces):
        part = pl.ds(piece * per_piece * chunk, per_piece * chunk)
        gets.append(
            (
                pltpu.make_async_copy(gradient_ref.at[:, part], gradient_tile.at[:, part], sems.at[piece, 0]),
                pltpu.make_async_copy(error_ref.at[:, part], error_tile.at[:, part], sems.at[piece, 1]),
            )
        )
    warm_get = pltpu.make_async_copy(warm_ref, warm_tile, sems.at[0, 2])
    warm_get.start()
    for pair in gets:
        pair[0].start()
        pair[1].start()
    warm_get.wait()
    packed = jnp.concatenate(
        [warm_tile[i : i + extra] for i in range(0, rank, extra)], axis=1
    ).astype(BF16)
    for piece in range(pieces):
        gets[piece][0].wait()
        gets[piece][1].wait()
        for peer in range(piece * per_piece, (piece + 1) * per_piece):
            for i in range(chunk // LANES):
                part = slice(peer * chunk + i * LANES, peer * chunk + (i + 1) * LANES)
                tile = gradient_tile[:, part].astype(F32) + error_tile[:, part].astype(F32)
                send_ref[peer, i * width : (i + 1) * width, :] = tile.astype(BF16)
            send_ref[peer, tall - extra :, :] = packed


def rows_kernel(groups, width, scale, got_ref, mean_ref, send_ref):
    peers, tall, _ = got_ref.shape
    chunk = mean_ref.shape[1]
    high = width * chunk // LANES
    replicas = peers // groups
    warm = []
    for group in range(groups):
        total = got_ref[group, 0:high, :].astype(F32)
        for replica in range(1, replicas):
            total += got_ref[replica * groups + group, 0:high, :].astype(F32)
        total *= scale
        for i in range(chunk // LANES):
            mean_ref[group * width : (group + 1) * width, i * LANES : (i + 1) * LANES] = total[
                i * width : (i + 1) * width
            ]
        packed = got_ref[group, high:, :].astype(F32)
        warm.append(
            jnp.concatenate([packed[:, i : i + width] for i in range(0, LANES, width)], axis=0)
        )
    rows = jnp.dot(
        jnp.concatenate(warm, axis=1), mean_ref[...], precision=HIGHEST, preferred_element_type=F32
    ).astype(BF16)
    for peer in range(send_ref.shape[0]):
        send_ref[peer] = rows


def add(got_ref):
    total = got_ref[0].astype(F32)
    for peer in range(1, got_ref.shape[0]):
        total += got_ref[peer].astype(F32)
    return total.astype(BF16)


def pack_gram(gram):
    half = gram.shape[0] // 2
    first, cross, second = gram[:half, :half], gram[:half, half:], gram[half:, half:]
    line = lax.broadcasted_iota(jnp.int32, (half, half), 0)
    lane = lax.broadcasted_iota(jnp.int32, (half, half), 1)
    diagonal = jnp.sum(jnp.where(line == lane, second, 0.0), axis=1, keepdims=True)
    return jnp.concatenate([jnp.where(line <= lane, first, second), diagonal, cross], axis=1)


def unpack_gram(packed):
    half = packed.shape[0]
    line = lax.broadcasted_iota(jnp.int32, (half, half), 0)
    lane = lax.broadcasted_iota(jnp.int32, (half, half), 1)
    both, diagonal, cross = packed[:, :half], packed[:, half : half + 1], packed[:, half + 1 :]
    first = jnp.where(line <= lane, both, 0.0)
    second = jnp.where(line > lane, both, jnp.where(line == lane, diagonal, 0.0))
    once = jnp.concatenate(
        [
            jnp.concatenate([first, cross], axis=1),
            jnp.concatenate([jnp.zeros((half, half), F32), second], axis=1),
        ],
        axis=0,
    )
    line = lax.broadcasted_iota(jnp.int32, (2 * half, 2 * half), 0)
    eye = line == lax.broadcasted_iota(jnp.int32, (2 * half, 2 * half), 1)
    return jnp.where(eye, once, once + once.T)


def columns_kernel(groups, got_ref, mean_ref, send_ref):
    rank, chunk = got_ref.shape[1:]
    half = rank // 2
    replicas = send_ref.shape[0] // groups
    rows = add(got_ref)
    across = (((1,), (1,)), ((), ()))
    product = lax.dot_general(
        rows.astype(F32), mean_ref[...], across, precision=HIGHEST, preferred_element_type=F32
    )
    gram = lax.dot_general(rows, rows, across, preferred_element_type=F32)
    pieces = jnp.concatenate(split(pack_gram(gram), 3), axis=1)[:, : 3 * rank].astype(F32)
    rows = rows.astype(F32)
    share, block = rank // replicas, chunk // (half * replicas // rank)
    lower = []
    for replica in range(replicas):
        mine = rows[replica * share : (replica + 1) * share]
        mine = jnp.concatenate([mine[:, i : i + block] for i in range(0, chunk, block)], axis=0)
        lower.append(jnp.concatenate([pieces, mine], axis=1).astype(BF16))
    width = product.shape[1] // groups
    for group in range(groups):
        high, low = split(product[:, group * width : (group + 1) * width], 2)
        upper = jnp.concatenate([high[:half], high[half:], low[:half], low[half:]], axis=1)
        for replica in range(replicas):
            peer = replica * groups + group
            send_ref[peer, 0:half, :] = upper
            send_ref[peer, half:rank, :] = lower[replica]


def eliminate(gram, product):
    rank, width = product.shape
    columns = [
        jnp.broadcast_to(gram[8 * (j // 8) :, j : j + 1], (rank - 8 * (j // 8), LANES))
        for j in range(rank)
    ]
    line = lax.broadcasted_iota(jnp.int32, (rank, LANES), 0)
    lane = lax.broadcasted_iota(jnp.int32, (rank, LANES), 1)
    work = jnp.concatenate([product, jnp.zeros((rank, LANES - width), F32)], axis=1)
    work = jnp.where(lane == line + width, 1.0, work)
    for k in range(rank):
        top = 8 * (k // 8)
        column = columns[k]
        inverse_root = lax.rsqrt(column[k - top : k - top + 1])
        column = column * inverse_root
        for j in range(k + 1, rank):
            first = 8 * (j // 8) - top
            columns[j] = columns[j] - column[first:] * column[j - top : j - top + 1]
        row = work[k : k + 1] * inverse_root
        rest = work[top:] - jnp.where(line[top:] > k, column, 0.0) * row
        rest = jnp.where(line[top:] == k, row, rest)
        work = jnp.concatenate([work[:top], rest], axis=0) if top else rest
    return work[:, width : width + rank], work[:, :width]


def factor_kernel(got_ref, next_ref, mix_ref, norm_ref, share_ref):
    rank, width = next_ref.shape
    half = rank // 2
    peers, _, chunk = got_ref.shape
    share = share_ref.shape[0]
    for peer in range(peers):
        mine = got_ref[peer, half:rank, 3 * rank :].astype(F32)
        mine = jnp.concatenate([mine[i : i + share] for i in range(0, half, share)], axis=1)
        share_ref[:, peer * chunk : (peer + 1) * chunk] = mine.astype(BF16)
    sums = [got_ref[peer].astype(F32) for peer in range(peers)]
    while len(sums) > 1:
        sums = [sum(sums[i + 1 : i + 2], sums[i]) for i in range(0, len(sums), 2)]
    upper, lower = sums[0][:half], sums[0][half:]
    upper = upper[:, : 2 * width] + upper[:, 2 * width :]
    product = jnp.concatenate([upper[:, :width], upper[:, width:]], axis=0)
    third = jnp.concatenate(
        [lower[:, 2 * rank + 2 : 3 * rank], jnp.zeros((half, 3), F32)], axis=1
    )
    gram = unpack_gram(lower[:, : rank + 1] + lower[:, rank + 1 : 2 * rank + 2] + third)
    line = lax.broadcasted_iota(jnp.int32, (rank, rank), 0)
    eye = (line == lax.broadcasted_iota(jnp.int32, (rank, rank), 1)).astype(F32)
    trace = jnp.sum(gram * eye)
    inverse, next_factor = eliminate(gram + (0.0001 * trace / rank) * eye, product)
    next_ref[...] = next_factor
    norm_ref[...] = jnp.full(norm_ref.shape, jnp.sum(next_factor * next_factor), F32)
    mix = lax.dot_general(
        next_factor,
        inverse,
        (((0,), (0,)), ((), ())),
        precision=HIGHEST,
        preferred_element_type=F32,
    )
    mix_ref[...] = jnp.concatenate(
        [*split(mix, 3), jnp.zeros((width, LANES - 3 * rank), BF16)], axis=1
    )


def update_kernel(
    norm_limit, norms_ref, shares_ref, mix_ref, gradient_ref, error_ref, applied_ref, next_ref, applied_tile, next_tile, sems
):
    width, row_count = next_ref.shape
    rank = shares_ref.shape[0] * shares_ref.shape[1]
    mix = mix_ref[...][:, : 3 * rank]
    norm_sq = jnp.sum(norms_ref[...][:, 0:1], axis=0, keepdims=True)
    clip_scale = jnp.minimum(1.0, norm_limit * lax.rsqrt(norm_sq + 1e-06))
    pieces = sems.shape[0]
    span = row_count // pieces
    step = min(512, span)
    puts = []
    for piece in range(pieces):
        for start in range(piece * span, (piece + 1) * span, step):
            part = slice(start, start + step)
            rows = jnp.concatenate(
                [shares_ref[i, :, part].astype(F32) for i in range(shares_ref.shape[0])], axis=0
            ).astype(BF16)
            decompressed = jnp.dot(
                mix, jnp.concatenate([rows, rows, rows], axis=0), preferred_element_type=F32
            )
            applied_tile[:, part] = (clip_scale * decompressed).astype(BF16)
            tile = (gradient_ref[:, part].astype(F32) + error_ref[:, part].astype(F32)).astype(BF16)
            next_tile[:, part] = (tile.astype(F32) - decompressed).astype(BF16)
        part = pl.ds(piece * span, span)
        for i, (source, target) in enumerate(((applied_tile, applied_ref), (next_tile, next_ref))):
            put = pltpu.make_async_copy(source.at[:, part], target.at[:, part], sems.at[piece, i])
            put.start()
            puts.append(put)
    for put in puts:
        put.wait()


def call(kernel, outs, *args, vmem=16, spaces=None, out_space=pltpu.VMEM, scratch=(), cost=None):
    spaces = spaces or [pltpu.VMEM] * len(args)
    return pl.pallas_call(
        kernel,
        out_shape=outs,
        in_specs=[pl.BlockSpec(memory_space=space) for space in spaces],
        out_specs=jax.tree.map(lambda _: pl.BlockSpec(memory_space=out_space), outs),
        scratch_shapes=scratch,
        compiler_params=pltpu.CompilerParams(vmem_limit_bytes=vmem * 1024 * 1024),
        cost_estimate=cost,
    )(*args)


def per_device(gradient, error_buffer, warm_factor):
    shape = jax.ShapeDtypeStruct
    replicas, far, near, groups = (lax.axis_size(axis) for axis in ("gx", "far", "near", "gz"))
    plane, groups, columns = ("gx", "near", "gz"), near * groups, far * near * groups
    gradient, error_buffer = gradient[0], error_buffer[0]
    width, row_count = gradient.shape
    rank = warm_factor.shape[0]
    peers = replicas * groups
    chunk = row_count // peers
    norm_limit = 0.1 * math.sqrt(width * columns * row_count)
    pieces = min(2, peers)
    message = shape((peers, (width * chunk + rank * width) // LANES, LANES), BF16)

    send = call(
        merge_kernel,
        message,
        *(
            pltpu.with_memory_space_constraint(x, pltpu.HBM)
            for x in (gradient, error_buffer, warm_factor)
        ),
        spaces=[pltpu.HBM] * 3,
        scratch=[
            pltpu.VMEM((width, row_count), BF16),
            pltpu.VMEM((width, row_count), BF16),
            pltpu.VMEM((rank, width), F32),
            pltpu.SemaphoreType.DMA((pieces, 3)),
        ],
    )
    got = lax.all_to_all(send, plane, 0, 0)
    mean, send = call(
        lambda *refs: rows_kernel(groups, width, 1.0 / replicas, *refs),
        (shape((groups * width, chunk), F32), shape((far, rank, chunk), BF16)),
        got,
    )
    got = lax.all_to_all(send, "far", 0, 0)
    message = shape((peers, rank, LANES), BF16)
    send = call(lambda *refs: columns_kernel(groups, *refs), message, got, mean)
    got = lax.all_to_all(send, plane, 0, 0)
    next_factor, mix, norm, share = call(
        factor_kernel,
        (
            shape((rank, width), F32),
            shape((width, LANES), BF16),
            shape((columns, LANES), F32),
            shape((rank // replicas, row_count), BF16),
        ),
        got,
    )
    norms = lax.all_to_all(norm, ("far", "near", "gz"), 0, 0, tiled=True)
    shares = lax.all_gather(share, "gx")
    applied, next_error = call(
        lambda *refs: update_kernel(norm_limit, *refs),
        (shape((width, row_count), BF16), shape((width, row_count), BF16)),
        norms,
        shares,
        mix,
        gradient,
        error_buffer,
        out_space=pl.ANY,
        scratch=[
            pltpu.VMEM((width, row_count), BF16),
            pltpu.VMEM((width, row_count), BF16),
            pltpu.SemaphoreType.DMA((8, 2)),
        ],
    )
    return applied, next_error[None], next_factor


def solution(mesh):
    replicas, depth, groups = (mesh.shape[axis] for axis in ("gx", "gy", "gz"))
    near = math.gcd(depth, 2)
    fine = jax.sharding.Mesh(
        mesh.devices.reshape(replicas, depth // near, near, groups), ("gx", "far", "near", "gz")
    )
    columns = ("far", "near", "gz")
    in_specs = (P("gx", columns, None), P("gx", columns, None), P(None, columns))
    out_specs = (P(columns, None), P("gx", columns, None), P(None, columns))
    return jax.shard_map(
        per_device, mesh=fine, in_specs=in_specs, out_specs=out_specs, check_vma=False
    )
```
